512 devices in a mesh: pb: 8 (over z), kv: 8 (over x, y_lo), ha: 8 (over y_hi, core).
Axes of the slice: x: 4, y: 8 (y_hi: 4, y_lo: 2; y = y_hi * 2 + y_lo), z: 8, core: 2. Of those that a mesh axis runs over, the one named last changes fastest.
Arguments:
- queries: bfloat16 [16384, 8192], P(('pb', 'kv', 'ha')), may hold values from -15 to 15
- keyvals: bfloat16 [2, 16384, 1024], P(None, ('pb', 'kv', 'ha')), may hold values from -6 to 6
- block_index: int32 [128, 16], P(('pb', 'kv')), may hold values from 0 to 127, as said below
- block_count: int32 [128], P(('pb', 'kv')), may hold values from 1 to 16, as said below
Outputs:
- attended: bfloat16 [16384, 8192], P(('pb', 'kv', 'ha'))
The draws below stay inside these ranges and needn't reach their ends.
Inputs may be any that keep to these rules, and one draw needn't show every extreme that they name: `block_index`: row i lists block_count[i] distinct blocks: first i, then i - 1 down to i - 2 where these are 0 or more, then blocks j <= i - 3 with j % 2 == 0, the largest such j first whenever one exists; the slots past the count hold i. `block_count`: some row uses all 16 slots.
All inputs are finite; a program needn't handle non-finite values.
Results may differ from the reference program's by a relative error of at most 0.0035.
Values may be sent and summed in bfloat16 or wider, within the bound.
No kernel may reach another device: no remote copies, remote signals or barrier semaphores. Data moves between devices by JAX's collectives and lax.ppermute only.
A program may use at most 64 MiB of HBM per device.

```python
import math
import jax
import jax.numpy as jnp
from jax import lax

QUERY_HEADS = 64
KEY_VALUE_HEADS = 8
HEAD_SIZE = 128
BLOCK_POSITIONS = 128
LOCAL = 3
MAXB = 16
SEQUENCE_LENGTH = 16384
SEQUENCE_BLOCKS = 128
STRIDE = 2


def shared_draw(key):
    subkeys = jax.random.split(key, 2)
    feature_columns = KEY_VALUE_HEADS * HEAD_SIZE
    normal_part = jax.random.normal(subkeys[1], (SEQUENCE_LENGTH, feature_columns), jnp.float32)
    return normal_part


def draw_keyvals(key, part):
    normal_part = shared_draw(key)
    key = jax.random.fold_in(key, 3)
    key_row_matrix = jnp.clip(normal_part, -6.0, 6.0)
    value_row_matrix = jnp.clip(jax.random.normal(key, (SEQUENCE_LENGTH, KEY_VALUE_HEADS * HEAD_SIZE), jnp.float32), -6.0, 6.0)
    return jnp.stack([key_row_matrix, value_row_matrix]).astype(jnp.bfloat16)


def draw_queries(key, part):
    key = jax.random.fold_in(key, 4)
    query_rows = jnp.clip(2.0 * jax.random.normal(key, (SEQUENCE_LENGTH, QUERY_HEADS * HEAD_SIZE), jnp.float32), -12.0, 12.0)
    return query_rows.astype(jnp.bfloat16)


def block_pattern(key):
    key = jax.random.fold_in(key, 5)
    subkeys = jax.random.split(key, 2)
    strided_total = SEQUENCE_BLOCKS // STRIDE
    spare = MAXB - LOCAL
    block_ids = jnp.arange(SEQUENCE_BLOCKS, dtype=jnp.int32)
    candidate = jnp.arange(strided_total, dtype=jnp.int32) * STRIDE
    usable = candidate[None, :] <= block_ids[:, None] - LOCAL
    usable_count = jnp.sum(usable.astype(jnp.int32), axis=1)
    ranks = jax.random.randint(subkeys[0], (SEQUENCE_BLOCKS, strided_total), 0, 1 << 20, jnp.int32)
    column = jnp.arange(strided_total, dtype=jnp.int32)[None, :]
    ranks = jnp.where(usable, ranks * strided_total + column + 1, (1 << 30) + column)
    newest = column == usable_count[:, None] - 1
    ranks = jnp.where(newest & usable, 0, ranks)
    order = jnp.argsort(ranks, axis=1)[:, :spare]
    chosen = candidate[order]
    wanted = jax.random.randint(subkeys[1], (SEQUENCE_BLOCKS,), spare // 2, spare + 1, jnp.int32)
    wanted = jnp.maximum(wanted, 1)
    wanted = jnp.where(block_ids == SEQUENCE_BLOCKS - 1, spare, wanted)
    strided_count = jnp.minimum(usable_count, wanted)
    local_count = jnp.minimum(LOCAL, block_ids + 1)
    slot_ids = jnp.arange(MAXB, dtype=jnp.int32)[None, :]
    near_entry = block_ids[:, None] - slot_ids
    far_slot = jnp.clip(slot_ids - local_count[:, None], 0, spare - 1)
    far_entry = jnp.take_along_axis(chosen, far_slot, axis=1)
    is_near = slot_ids < local_count[:, None]
    is_far = (slot_ids >= local_count[:, None]) & (slot_ids < (local_count + strided_count)[:, None])
    listing = jnp.where(is_near, near_entry, jnp.where(is_far, far_entry, block_ids[:, None]))
    return (listing.astype(jnp.int32), (local_count + strided_count).astype(jnp.int32))


def draw_block_index(key, part):
    listing, counted = block_pattern(key)
    return listing


def draw_block_count(key, part):
    listing, counted = block_pattern(key)
    return counted


def setup_inputs(seed: int = 0) -> dict:
    streams_of = jax.random.split(jax.random.key(seed), 5)
    return {
        "queries": draw_queries(jax.random.fold_in(streams_of[4], 71), 0),
        "keyvals": draw_keyvals(jax.random.fold_in(streams_of[4], 71), 0),
        "block_index": draw_block_index(jax.random.fold_in(streams_of[4], 71), 0),
        "block_count": draw_block_count(jax.random.fold_in(streams_of[4], 71), 0),
    }


def reference(queries, keyvals, block_index, block_count):
    query_head_group = QUERY_HEADS // KEY_VALUE_HEADS
    score_scale = 1.0 / math.sqrt(HEAD_SIZE)
    blocked_keys = keyvals[0].reshape(SEQUENCE_BLOCKS, BLOCK_POSITIONS, KEY_VALUE_HEADS, HEAD_SIZE)
    blocked_values = keyvals[1].reshape(SEQUENCE_BLOCKS, BLOCK_POSITIONS, KEY_VALUE_HEADS, HEAD_SIZE)
    query_blocks = queries.reshape(SEQUENCE_BLOCKS, BLOCK_POSITIONS, KEY_VALUE_HEADS, query_head_group, HEAD_SIZE)
    positions = jnp.arange(BLOCK_POSITIONS, dtype=jnp.int32)
    slot_ids = jnp.arange(MAXB, dtype=jnp.int32)

    def one_block(inputs):
        query_rows, listed, listed_count, block_number = inputs
        key_row_matrix = blocked_keys[listed].astype(jnp.float32)
        value_row_matrix = blocked_values[listed].astype(jnp.float32)
        scores = jnp.einsum('rgzd,ecgd->gzrec', query_rows.astype(jnp.float32), key_row_matrix) * score_scale
        slot_ok = (slot_ids < listed_count)[None, :, None]
        earlier = (listed < block_number)[None, :, None]
        causal = positions[None, None, :] <= positions[:, None, None]
        allowed = slot_ok & (earlier | causal)
        peak = lax.optimization_barrier(jnp.max(jnp.where(allowed, scores, -1e+30), axis=(3, 4)))
        weights = jnp.where(allowed, jnp.exp(scores - peak[..., None, None]), 0.0)
        totals = lax.optimization_barrier(jnp.sum(weights, axis=(3, 4)))
        rounded = lax.optimization_barrier(weights.astype(jnp.bfloat16))
        numerator = jnp.einsum('gzrec,ecgd->rgzd', rounded.astype(jnp.float32), value_row_matrix)
        output = numerator / jnp.transpose(totals, (2, 0, 1))[..., None]
        return output.astype(jnp.bfloat16).reshape(BLOCK_POSITIONS, QUERY_HEADS * HEAD_SIZE)
    block_ids = jnp.arange(SEQUENCE_BLOCKS, dtype=jnp.int32)
    result = lax.map(one_block, (query_blocks, block_index, block_count, block_ids))
    return result.reshape(SEQUENCE_LENGTH, QUERY_HEADS * HEAD_SIZE)
```

```python
import math

import jax
import jax.numpy as jnp
from jax import lax
from jax.experimental import pallas as pl
from jax.experimental.pallas import tpu as pltpu
from jax.sharding import Mesh, PartitionSpec as P

HEAD_SIZE = 128
BLOCK_POSITIONS = 128
MAXB = 16
KEYS = MAXB * BLOCK_POSITIONS
HALF = BLOCK_POSITIONS // 2
STRIP = 32
GROUP = 8
ROWS = GROUP * STRIP
ODD = 3
NEGATIVE = -1e30
FACTOR = math.log2(math.e) / math.sqrt(HEAD_SIZE)
Z, X, YLO, YHI, CORE = "z", "x", "ylo", "yhi", "core"
RING = (YLO, YHI)


def attend(meta, lists, other_lists, q_ref, *refs):
    columns, odds = refs[:10], refs[10:12]
    out_ref, table, keys, values, scores, weights, sems = refs[12:]
    z, x, ylo, core = meta[0], meta[1], meta[2], meta[3]
    evens = table.shape[1] - ODD
    per_column = evens // 4
    copies = []

    def bring(source, target):
        copy = pltpu.make_async_copy(source, target, sems.at[len(copies)])
        copy.start()
        copies.append(copy)

    for rc in range(2):
        own, left, right, far_a, far_b = columns[rc * 5 : rc * 5 + 5]
        bring(own, table.at[rc, pl.ds(0, per_column)])
        bring(right, table.at[rc, pl.ds(per_column, per_column)])
        bring(far_a, table.at[rc, pl.ds(2 * per_column, per_column // 2)])
        bring(far_b, table.at[rc, pl.ds(2 * per_column + per_column // 2, per_column // 2)])
        bring(left, table.at[rc, pl.ds(3 * per_column, per_column)])
        bring(odds[rc], table.at[rc, pl.ds(evens, ODD)])
    for copy in copies:
        copy.wait()

    pair = z * 4 + x
    cell = lax.broadcasted_iota(jnp.int32, (ROWS, BLOCK_POSITIONS), 1)
    row = lax.broadcasted_iota(jnp.int32, (ROWS, BLOCK_POSITIONS), 0)
    cell_core = jnp.bitwise_xor(cell // HALF, core)
    key_position = (cell % HALF) // STRIP * HALF + cell_core * STRIP + cell % STRIP
    row_position = core * STRIP + row % STRIP

    def one_block(b, carry):
        mine = (b // 2) == ylo
        inside = b % 2
        count = jnp.where(mine, lists[inside, MAXB], other_lists[inside, MAXB])
        for e in range(MAXB):
            j = jnp.where(mine, lists[inside, e], other_lists[inside, e])
            relative = jnp.bitwise_and(j // 4 - x, 3)
            even_row = relative * per_column + (j // 16) * 2 + (j // 2) % 2
            odd_row = evens + jnp.clip((j - 4 * pair + 1) // 2, 0, ODD - 1)
            t = jnp.where(j % 2 == 0, even_row, odd_row)
            for rc in range(2):
                span = pl.ds(e * BLOCK_POSITIONS + rc * HALF, HALF)
                keys[span, :] = table[rc, t, 0]
                values[span, :] = table[rc, t, 1]
        for strip in range(2):
            source = 2 * b + strip
            q = jnp.concatenate(
                [q_ref[source, :, h * HEAD_SIZE : (h + 1) * HEAD_SIZE] for h in range(GROUP)], axis=0
            )
            peak = jnp.full((ROWS, BLOCK_POSITIONS), NEGATIVE, jnp.float32)
            for g in range(MAXB // 2):
                s = lax.dot_general(
                    q,
                    keys[g * 256 : (g + 1) * 256, :],
                    (((1,), (1,)), ((), ())),
                    preferred_element_type=jnp.float32,
                )
                for half in range(2):
                    e = 2 * g + half
                    part = s[:, half * 128 : (half + 1) * 128]
                    if e == 0:
                        part = jnp.where(key_position <= row_position + strip * HALF, part, NEGATIVE)
                    else:
                        part = jnp.where(e < count, part, NEGATIVE)
                    scores[strip, :, e * 128 : (e + 1) * 128] = part
                    peak = jnp.maximum(peak, part)
            top = jnp.max(peak, axis=1, keepdims=True) * FACTOR
            total = jnp.zeros((ROWS, BLOCK_POSITIONS), jnp.float32)
            for e in range(MAXB):
                span = slice(e * 128, (e + 1) * 128)
                w = jnp.exp2(scores[strip, :, span] * FACTOR - top)
                total = total + w
                weights[strip, :, span] = w.astype(jnp.bfloat16)
            numerator = jnp.dot(weights[strip], values[...], preferred_element_type=jnp.float32)
            result = numerator / jnp.sum(total, axis=1, keepdims=True)
            result = result.astype(jnp.bfloat16)
            for h in range(GROUP):
                out_ref[source, :, h * HEAD_SIZE : (h + 1) * HEAD_SIZE] = result[h * STRIP : (h + 1) * STRIP]
        return carry

    lax.fori_loop(0, 4, one_block, 0)


def attention(meta, lists, other_lists, q, columns, odds, interpret=False):
    evens = 4 * columns[0].shape[0]
    smem = pl.BlockSpec(memory_space=pltpu.SMEM)
    vmem = pl.BlockSpec(memory_space=pltpu.VMEM)
    hbm = pl.BlockSpec(memory_space=pl.ANY)
    return pl.pallas_call(
        attend,
        out_shape=jax.ShapeDtypeStruct(q.shape, q.dtype),
        in_specs=[smem, smem, smem, vmem] + [hbm] * 12,
        out_specs=vmem,
        scratch_shapes=[
            pltpu.VMEM((2, evens + ODD, 2, HALF, HEAD_SIZE), jnp.bfloat16),
            pltpu.VMEM((KEYS, HEAD_SIZE), jnp.bfloat16),
            pltpu.VMEM((KEYS, HEAD_SIZE), jnp.bfloat16),
            pltpu.VMEM((2, ROWS, KEYS), jnp.float32),
            pltpu.VMEM((2, ROWS, KEYS), jnp.bfloat16),
            pltpu.SemaphoreType.DMA((12,)),
        ],
        compiler_params=pltpu.CompilerParams(vmem_limit_bytes=40 * 2**20),
        interpret=interpret,
    )(meta, lists, other_lists, q, *columns, *odds)


def shift(array, axis, by):
    size = lax.axis_size(axis)
    return lax.ppermute(array, axis, [(i, (i + by) % size) for i in range(size)])


def swap(array, axis):
    return lax.ppermute(array, axis, [(0, 1), (1, 0)])


def body(queries, keyvals, block_index, block_count):
    lists = jnp.concatenate([block_index, block_count[:, None]], axis=1)
    other_lists = swap(lists, YLO)
    meta = jnp.stack([lax.axis_index(a) for a in (Z, X, YLO, CORE)]).astype(jnp.int32)
    heads = lax.axis_size(RING)

    sent = keyvals.reshape(2, STRIP, heads, HEAD_SIZE).transpose(2, 0, 1, 3)
    local = lax.all_to_all(sent, RING, split_axis=0, concat_axis=0, tiled=True)
    local = local.reshape(4, 2, 2, STRIP, HEAD_SIZE).transpose(0, 2, 1, 3, 4)
    local = local.reshape(4, 2, HALF, HEAD_SIZE)

    summary = jnp.stack([local[0], local[2]])
    gathered = lax.all_gather(summary, Z, axis=0, tiled=True)
    sent_q = queries.reshape(STRIP, heads, GROUP * HEAD_SIZE).transpose(1, 0, 2)
    q = lax.all_to_all(sent_q, RING, split_axis=0, concat_axis=0, tiled=True)

    middle = gathered.shape[0] // 2
    left = shift(gathered, X, 1)
    right = shift(gathered, X, -1)
    far_a = shift(left[:middle], X, 1)
    far_b = shift(right[middle:], X, -1)
    pairs = lax.axis_size((Z, X))
    before = lax.ppermute(local[3], (Z, X), [(i, i + 1) for i in range(pairs - 1)])
    odd = jnp.stack([before, local[1], local[3]])

    columns = [gathered, left, right, far_a, far_b]
    columns += [swap(column, CORE) for column in columns]
    odds = [odd, swap(odd, CORE)]
    result = attention(meta, lists, other_lists, q, columns, odds)
    result = lax.all_to_all(result, RING, split_axis=0, concat_axis=0, tiled=True)
    return result.transpose(1, 0, 2).reshape(STRIP, heads * GROUP * HEAD_SIZE)


def solution(mesh):
    pb, kv, ha = mesh.devices.shape
    fine = Mesh(mesh.devices.reshape(pb, kv // 2, 2, ha // 2, 2), (Z, X, YLO, YHI, CORE))
    rows = (Z, X, YLO, YHI, CORE)
    shard = (Z, X, YLO)
    return jax.shard_map(
        body,
        mesh=fine,
        in_specs=(P(rows, None), P(None, rows, None), P(shard, None), P(shard)),
        out_specs=P(rows, None),
        check_vma=False,
    )
```

```python
import math

import jax
import jax.numpy as jnp
from jax import lax
from jax.experimental import pallas as pl
from jax.experimental.pallas import tpu as pltpu
from jax.sharding import Mesh, PartitionSpec as P

HEAD_SIZE = 128
BLOCK_POSITIONS = 128
MAXB = 16
KEYS = MAXB * BLOCK_POSITIONS
HALF = BLOCK_POSITIONS // 2
STRIP = 32
GROUP = 8
HALF_ROWS = GROUP * STRIP
ODD = 3
NEGATIVE = -1e30
FACTOR = math.log2(math.e) / math.sqrt(HEAD_SIZE)
Z, X, YLO, YHI, CORE = "z", "x", "ylo", "yhi", "core"
RING = (YLO, YHI)


def attend(meta, lists, other_lists, q_ref, *refs):
    columns, odds = refs[:8], refs[8:10]
    out_ref, table, qs, keys, values, scores, weights, sems = refs[10], refs[11], *(
        refs[12 + 2 * i : 14 + 2 * i] for i in range(4)
    ), refs[20], refs[21]
    z, x, ylo, core, me = (meta[i] for i in range(5))
    evens = table.shape[1] - ODD
    per_column = evens // 4
    copies = []

    def bring(source, target):
        copy = pltpu.make_async_copy(source, target, sems.at[len(copies)])
        copy.start()
        copies.append(copy)

    for rc in range(2):
        side = jnp.bitwise_xor(core, rc)
        for source, relative in zip(columns[rc * 4 : rc * 4 + 4], (0, 3 - 2 * side, 1 + 2 * side, 2)):
            bring(source, table.at[rc, pl.ds(relative * per_column, per_column)])
        bring(odds[rc], table.at[rc, pl.ds(evens, ODD)])
    for copy in copies:
        copy.wait()

    pair = z * 4 + x
    cell = lax.broadcasted_iota(jnp.int32, (HALF_ROWS, BLOCK_POSITIONS), 1)
    row = lax.broadcasted_iota(jnp.int32, (HALF_ROWS, BLOCK_POSITIONS), 0)
    cell_core = jnp.bitwise_xor(cell // HALF, core)
    key_position = (cell % HALF) // STRIP * HALF + cell_core * STRIP + cell % STRIP
    row_position = core * STRIP + row % STRIP

    def entry(b, e):
        return jnp.where(b // 2 == ylo, lists[b % 2, e], other_lists[b % 2, e])

    def prepare(b, slot):
        for e in range(MAXB):
            j = entry(b, e)
            relative = jnp.bitwise_and(j // 4 - x, 3)
            odd_row = evens + jnp.clip((j - 4 * pair + 1) // 2, 0, ODD - 1)
            for rc in range(2):
                upward = jnp.bitwise_and(z - j // 16, 7)
                distance = jnp.where(core == rc, upward, jnp.bitwise_and(8 - upward, 7))
                place = jnp.bitwise_and(distance, 1) * 4 + jnp.bitwise_and(distance, 2) + distance // 4
                even_row = relative * per_column + place * 2 + (j // 2) % 2
                t = jnp.where(j % 2 == 0, even_row, odd_row)
                span = pl.ds(e * BLOCK_POSITIONS + rc * HALF, HALF)
                keys[slot][span, :] = table[rc, t, 0]
                values[slot][span, :] = table[rc, t, 1]
        for strip in range(2):
            for h in range(GROUP):
                qs[slot][pl.ds((strip * GROUP + h) * STRIP, STRIP), :] = q_ref[
                    2 * b + strip, :, h * HEAD_SIZE : (h + 1) * HEAD_SIZE
                ]

    def score(slot, g, count):
        s = lax.dot_general(
            qs[slot][...],
            keys[slot][g * 256 : (g + 1) * 256, :],
            (((1,), (1,)), ((), ())),
            preferred_element_type=jnp.float32,
        )
        for e in (2 * g, 2 * g + 1):
            for strip in range(2):
                lines = slice(strip * HALF_ROWS, (strip + 1) * HALF_ROWS)
                part = s[lines, (e % 2) * 128 : (e % 2 + 1) * 128]
                keep = key_position <= row_position + strip * HALF if e == 0 else e < count
                scores[slot][lines, e * 128 : (e + 1) * 128] = jnp.where(keep, part, NEGATIVE)

    def finish(b, slot, later):
        for strip in range(2):
            lines = slice(strip * HALF_ROWS, (strip + 1) * HALF_ROWS)
            peak = scores[slot][lines, 0:128]
            for e in range(1, MAXB):
                peak = jnp.maximum(peak, scores[slot][lines, e * 128 : (e + 1) * 128])
            top = jnp.max(peak, axis=1, keepdims=True) * FACTOR
            total = jnp.zeros((HALF_ROWS, BLOCK_POSITIONS), jnp.float32)
            for e in range(MAXB):
                if e % 4 == 0 and later is not None:
                    score(1 - slot, strip * 4 + e // 4, later)
                span = slice(e * 128, (e + 1) * 128)
                w = jnp.exp2(scores[slot][lines, span] * FACTOR - top)
                total = total + w
                weights[lines, span] = w.astype(jnp.bfloat16)
            numerator = jnp.dot(weights[lines, :], values[slot][...], preferred_element_type=jnp.float32)
            result = (numerator / jnp.sum(total, axis=1, keepdims=True)).astype(jnp.bfloat16)
            place = jnp.bitwise_xor(2 * b + strip, me)
            for h in range(GROUP):
                out_ref[place, :, h * HEAD_SIZE : (h + 1) * HEAD_SIZE] = result[h * STRIP : (h + 1) * STRIP]

    prepare(0, 0)
    for g in range(MAXB // 2):
        score(0, g, entry(0, MAXB))

    def step(i, carry):
        b = 2 * i
        prepare(b + 1, 1)
        finish(b, 0, entry(b + 1, MAXB))
        after = jnp.minimum(b + 2, 3)
        prepare(after, 0)
        finish(b + 1, 1, entry(after, MAXB))
        return carry

    lax.fori_loop(0, 2, step, 0)


def attention(meta, lists, other_lists, q, columns, odds, interpret=False):
    evens = 4 * columns[0].shape[0]
    smem = pl.BlockSpec(memory_space=pltpu.SMEM)
    vmem = pl.BlockSpec(memory_space=pltpu.VMEM)
    hbm = pl.BlockSpec(memory_space=pl.ANY)
    return pl.pallas_call(
        attend,
        out_shape=jax.ShapeDtypeStruct(q.shape, q.dtype),
        in_specs=[smem, smem, smem, vmem] + [hbm] * 10,
        out_specs=vmem,
        scratch_shapes=[pltpu.VMEM((2, evens + ODD, 2, HALF, HEAD_SIZE), jnp.bfloat16)]
        + [pltpu.VMEM((2 * HALF_ROWS, HEAD_SIZE), jnp.bfloat16)] * 2
        + [pltpu.VMEM((KEYS, HEAD_SIZE), jnp.bfloat16)] * 4
        + [pltpu.VMEM((2 * HALF_ROWS, KEYS), jnp.float32)] * 2
        + [pltpu.VMEM((2 * HALF_ROWS, KEYS), jnp.bfloat16), pltpu.SemaphoreType.DMA((10,))],
        compiler_params=pltpu.CompilerParams(vmem_limit_bytes=40 * 2**20),
        cost_estimate=pl.CostEstimate(flops=2**31, bytes_accessed=8 * 2**20, transcendentals=2**22),
        interpret=interpret,
    )(meta, lists, other_lists, q, *columns, *odds)


def assemble_kernel(meta, *refs):
    out_ref = refs[-1]
    for k, ref in enumerate(refs[:-1]):
        column = jnp.bitwise_xor(meta[4], k) * ref.shape[1]
        out_ref[:, pl.ds(pl.multiple_of(column, ref.shape[1]), ref.shape[1])] = ref[...]


def assemble(meta, pieces, interpret=False):
    rows, width = pieces[0].shape
    vmem = pl.BlockSpec(memory_space=pltpu.VMEM)
    return pl.pallas_call(
        assemble_kernel,
        out_shape=jax.ShapeDtypeStruct((rows, width * len(pieces)), pieces[0].dtype),
        in_specs=[pl.BlockSpec(memory_space=pltpu.SMEM)] + [vmem] * len(pieces),
        out_specs=vmem,
        interpret=interpret,
    )(meta, *pieces)


def swap(array, axis):
    return lax.ppermute(array, axis, [(0, 1), (1, 0)])


def around(array, axis, by):
    size = lax.axis_size(axis)
    pairs = [(2 * i + c, 2 * ((i + (by, -by)[c]) % size) + c) for i in range(size) for c in range(2)]
    return lax.ppermute(array, (axis, CORE), pairs)


def body(queries, keyvals, block_index, block_count):
    lists = jnp.concatenate([block_index, block_count[:, None]], axis=1)
    other_lists = swap(lists, YLO)
    meta = jnp.stack([lax.axis_index(a) for a in (Z, X, YLO, CORE, RING)]).astype(jnp.int32)
    heads = lax.axis_size(RING)

    sent = keyvals.reshape(2, STRIP, heads, HEAD_SIZE).transpose(2, 0, 1, 3)
    local = lax.all_to_all(sent, RING, split_axis=0, concat_axis=0, tiled=True)
    local, queries = lax.optimization_barrier((local, queries))
    local = local.reshape(4, 2, 2, STRIP, HEAD_SIZE).transpose(0, 2, 1, 3, 4)
    local = local.reshape(4, 2, HALF, HEAD_SIZE)
    sent_q = queries.reshape(STRIP, heads, GROUP * HEAD_SIZE).transpose(1, 0, 2)
    q = lax.all_to_all(sent_q, RING, split_axis=0, concat_axis=0, tiled=True)
    pairs = lax.axis_size((Z, X))
    before = lax.ppermute(local[3], (Z, X), [(i, i + 1) for i in range(pairs - 1)])
    odd = jnp.stack([before, local[1], local[3]])
    other_odd = swap(odd, CORE)

    gathered = jnp.stack([local[0], local[2]])
    for by in (4, 2, 1):
        gathered = jnp.concatenate([gathered, around(gathered, Z, by)])

    first = around(gathered, X, 1)
    own_swapped = swap(gathered, CORE)
    first, gathered, other_odd, other_lists, own_swapped, q = lax.optimization_barrier(
        (first, gathered, other_odd, other_lists, own_swapped, q)
    )
    far = around(first, X, 1)
    second = around(gathered, X, -1)

    columns = [gathered, first, second, far, own_swapped]
    columns += [swap(column, CORE) for column in columns[1:4]]
    result = attention(meta, lists, other_lists, q, columns, [odd, other_odd])
    pieces = [result[0]]
    for k in range(1, heads):
        pieces.append(lax.ppermute(result[k], RING, [(i, i ^ k) for i in range(heads)]))
    return assemble(meta, pieces)


def solution(mesh):
    pb, kv, ha = mesh.devices.shape
    fine = Mesh(mesh.devices.reshape(pb, kv // 2, 2, ha // 2, 2), (Z, X, YLO, YHI, CORE))
    rows = (Z, X, YLO, YHI, CORE)
    shard = (Z, X, YLO)
    return jax.shard_map(
        body,
        mesh=fine,
        in_specs=(P(rows, None), P(None, rows, None), P(shard, None), P(shard)),
        out_specs=P(rows, None),
        check_vma=False,
    )
```

```python
import math

import jax
import jax.numpy as jnp
from jax import lax
from jax.experimental import pallas as pl
from jax.experimental.pallas import tpu as pltpu
from jax.sharding import Mesh, PartitionSpec as P

HEAD_SIZE = 128
BLOCK_POSITIONS = 128
MAXB = 16
KEYS = MAXB * BLOCK_POSITIONS
HALF = BLOCK_POSITIONS // 2
STRIP = 32
GROUP = 8
ROWS = GROUP * STRIP
ODD = 3
NEGATIVE = -1e30
FACTOR = math.log2(math.e) / math.sqrt(HEAD_SIZE)
Z, X, YLO, YHI, CORE = "z", "x", "ylo", "yhi", "core"
RING = (YLO, YHI)


def attend(meta, lists, other_lists, q_ref, even, other_even, odd, other_odd, out_ref, qs, keys, values, scores, weights):
    z, x, ylo, core = (meta[i] for i in range(4))
    pair = z * 4 + x
    cell = lax.broadcasted_iota(jnp.int32, (ROWS, BLOCK_POSITIONS), 1)
    row = lax.broadcasted_iota(jnp.int32, (ROWS, BLOCK_POSITIONS), 0)
    cell_core = jnp.bitwise_xor(cell // HALF, core)
    key_position = (cell % HALF) // STRIP * HALF + cell_core * STRIP + cell % STRIP
    row_position = core * STRIP + row % STRIP

    def one_block(b, carry):
        mine = (b // 2) == ylo
        inside = b % 2
        count = jnp.where(mine, lists[inside, MAXB], other_lists[inside, MAXB])
        for e in range(MAXB):
            j = jnp.where(mine, lists[inside, e], other_lists[inside, e])
            is_even = j % 2 == 0
            even_row = (j // 4) % 4 * (even.shape[0] // 4) + j // 16 * 2 + (j // 2) % 2
            odd_row = jnp.clip((j - 4 * pair + 1) // 2, 0, ODD - 1)
            for rc, (evens, odds) in enumerate(((even, odd), (other_even, other_odd))):
                span = pl.ds(e * BLOCK_POSITIONS + rc * HALF, HALF)
                keys[span, :] = jnp.where(is_even, evens[even_row, 0], odds[odd_row, 0])
                values[span, :] = jnp.where(is_even, evens[even_row, 1], odds[odd_row, 1])
        for strip in range(2):
            for h in range(GROUP):
                qs[pl.ds((strip * GROUP + h) * STRIP, STRIP), :] = q_ref[
                    2 * b + strip, :, h * HEAD_SIZE : (h + 1) * HEAD_SIZE
                ]
        for g in range(MAXB // 2):
            s = lax.dot_general(
                qs[...],
                keys[g * 256 : (g + 1) * 256, :],
                (((1,), (1,)), ((), ())),
                preferred_element_type=jnp.float32,
            )
            for e in (2 * g, 2 * g + 1):
                for strip in range(2):
                    lines = slice(strip * ROWS, (strip + 1) * ROWS)
                    part = s[lines, (e % 2) * 128 : (e % 2 + 1) * 128]
                    keep = key_position <= row_position + strip * HALF if e == 0 else e < count
                    scores[lines, e * 128 : (e + 1) * 128] = jnp.where(keep, part, NEGATIVE)
        for strip in range(2):
            lines = slice(strip * ROWS, (strip + 1) * ROWS)
            peak = scores[lines, 0:128]
            for e in range(1, MAXB):
                peak = jnp.maximum(peak, scores[lines, e * 128 : (e + 1) * 128])
            top = jnp.max(peak, axis=1, keepdims=True) * FACTOR
            total = jnp.zeros((ROWS, BLOCK_POSITIONS), jnp.float32)
            for e in range(MAXB):
                span = slice(e * 128, (e + 1) * 128)
                w = jnp.exp2(scores[lines, span] * FACTOR - top)
                total = total + w
                weights[lines, span] = w.astype(jnp.bfloat16)
            numerator = jnp.dot(weights[lines, :], values[...], preferred_element_type=jnp.float32)
            result = (numerator / jnp.sum(total, axis=1, keepdims=True)).astype(jnp.bfloat16)
            for h in range(GROUP):
                out_ref[2 * b + strip, :, h * HEAD_SIZE : (h + 1) * HEAD_SIZE] = result[h * STRIP : (h + 1) * STRIP]
        return carry

    lax.fori_loop(0, 4, one_block, 0)


def attention(meta, lists, other_lists, q, even, other_even, odd, other_odd, interpret=False):
    smem = pl.BlockSpec(memory_space=pltpu.SMEM)
    vmem = pl.BlockSpec(memory_space=pltpu.VMEM)
    return pl.pallas_call(
        attend,
        out_shape=jax.ShapeDtypeStruct(q.shape, q.dtype),
        in_specs=[smem, smem, smem] + [vmem] * 5,
        out_specs=vmem,
        scratch_shapes=[
            pltpu.VMEM((2 * ROWS, HEAD_SIZE), jnp.bfloat16),
            pltpu.VMEM((KEYS, HEAD_SIZE), jnp.bfloat16),
            pltpu.VMEM((KEYS, HEAD_SIZE), jnp.bfloat16),
            pltpu.VMEM((2 * ROWS, KEYS), jnp.float32),
            pltpu.VMEM((2 * ROWS, KEYS), jnp.bfloat16),
        ],
        compiler_params=pltpu.CompilerParams(vmem_limit_bytes=40 * 2**20),
        cost_estimate=pl.CostEstimate(flops=2**31, bytes_accessed=8 * 2**20, transcendentals=2**22),
        interpret=interpret,
    )(meta, lists, other_lists, q, even, other_even, odd, other_odd)


def swap(array, axis):
    return lax.ppermute(array, axis, [(0, 1), (1, 0)])


def body(queries, keyvals, block_index, block_count):
    lists = jnp.concatenate([block_index, block_count[:, None]], axis=1)
    meta = jnp.stack([lax.axis_index(a) for a in (Z, X, YLO, CORE)]).astype(jnp.int32)
    heads = lax.axis_size(RING)

    sent = keyvals.reshape(2, STRIP, heads, HEAD_SIZE).transpose(2, 0, 1, 3)
    local = lax.all_to_all(sent, RING, split_axis=0, concat_axis=0, tiled=True)
    local = local.reshape(4, 2, 2, STRIP, HEAD_SIZE).transpose(0, 2, 1, 3, 4)
    local = local.reshape(4, 2, HALF, HEAD_SIZE)

    summary = jnp.stack([local[0], local[2]])
    copies = jnp.broadcast_to(summary[None], (lax.axis_size(Z),) + summary.shape)
    column = lax.all_to_all(copies, Z, split_axis=0, concat_axis=0, tiled=True)
    column = column.reshape((-1,) + summary.shape[1:])
    even = lax.all_gather(column, X, axis=0, tiled=True)

    queries, local, lists = lax.optimization_barrier((queries, local, lists, column))[:3]
    sent_q = queries.reshape(STRIP, heads, GROUP * HEAD_SIZE).transpose(1, 0, 2)
    q = lax.all_to_all(sent_q, RING, split_axis=0, concat_axis=0, tiled=True)
    other_lists = swap(lists, YLO)
    pairs = lax.axis_size((Z, X))
    before = lax.ppermute(local[3], (Z, X), [(i, i + 1) for i in range(pairs - 1)])
    odd = jnp.stack([before, local[1], local[3]])
    other_odd = swap(odd, CORE)
    even, q, other_lists, odd, other_odd = lax.optimization_barrier((even, q, other_lists, odd, other_odd))

    result = attention(meta, lists, other_lists, q, even, swap(even, CORE), odd, other_odd)
    result = lax.all_to_all(result, RING, split_axis=0, concat_axis=0, tiled=True)
    return result.transpose(1, 0, 2).reshape(STRIP, heads * GROUP * HEAD_SIZE)


def solution(mesh):
    pb, kv, ha = mesh.devices.shape
    fine = Mesh(mesh.devices.reshape(pb, kv // 2, 2, ha // 2, 2), (Z, X, YLO, YHI, CORE))
    rows = (Z, X, YLO, YHI, CORE)
    shard = (Z, X, YLO)
    return jax.shard_map(
        body,
        mesh=fine,
        in_specs=(P(rows, None), P(None, rows, None), P(shard, None), P(shard)),
        out_specs=P(rows, None),
        check_vma=False,
    )
```

```python
import math

import jax
import jax.numpy as jnp
from jax import lax
from jax.experimental import pallas as pl
from jax.experimental.pallas import tpu as pltpu
from jax.sharding import Mesh, PartitionSpec as P

HEAD_SIZE = 128
BLOCK_POSITIONS = 128
MAXB = 16
KEYS = MAXB * BLOCK_POSITIONS
HALF = BLOCK_POSITIONS // 2
STRIP = 32
GROUP = 8
ROWS = GROUP * STRIP
ODD = 3
NEGATIVE = -1e30
FACTOR = math.log2(math.e) / math.sqrt(HEAD_SIZE)
Z, X, YLO, YHI, CORE = "z", "x", "ylo", "yhi", "core"
RING = (YLO, YHI)


def attend(meta, lists, other_lists, q_ref, even, other_even, odd, other_odd, out_ref, qs, keys, values, scores, weights):
    z, x, ylo, core = (meta[i] for i in range(4))
    pair = z * 4 + x
    cell = lax.broadcasted_iota(jnp.int32, (ROWS, BLOCK_POSITIONS), 1)
    row = lax.broadcasted_iota(jnp.int32, (ROWS, BLOCK_POSITIONS), 0)
    cell_core = jnp.bitwise_xor(cell // HALF, core)
    key_position = (cell % HALF) // STRIP * HALF + cell_core * STRIP + cell % STRIP
    row_position = core * STRIP + row % STRIP

    def one_block(b, carry):
        mine = (b // 2) == ylo
        inside = b % 2
        count = jnp.where(mine, lists[inside, MAXB], other_lists[inside, MAXB])
        for e in range(MAXB):
            j = jnp.where(mine, lists[inside, e], other_lists[inside, e])
            is_even = j % 2 == 0
            even_row = j // 2
            odd_row = jnp.clip((j - 4 * pair + 1) // 2, 0, ODD - 1)
            for rc, (evens, odds) in enumerate(((even, odd), (other_even, other_odd))):
                span = pl.ds(e * BLOCK_POSITIONS + rc * HALF, HALF)
                keys[span, :] = jnp.where(is_even, evens[even_row, 0], odds[odd_row, 0])
                values[span, :] = jnp.where(is_even, evens[even_row, 1], odds[odd_row, 1])
        for strip in range(2):
            for h in range(GROUP):
                qs[pl.ds((strip * GROUP + h) * STRIP, STRIP), :] = q_ref[
                    2 * b + strip, :, h * HEAD_SIZE : (h + 1) * HEAD_SIZE
                ]
        for g in range(MAXB // 2):
            s = lax.dot_general(
                qs[...],
                keys[g * 256 : (g + 1) * 256, :],
                (((1,), (1,)), ((), ())),
                preferred_element_type=jnp.float32,
            )
            for e in (2 * g, 2 * g + 1):
                for strip in range(2):
                    lines = slice(strip * ROWS, (strip + 1) * ROWS)
                    part = s[lines, (e % 2) * 128 : (e % 2 + 1) * 128]
                    keep = key_position <= row_position + strip * HALF if e == 0 else e < count
                    scores[lines, e * 128 : (e + 1) * 128] = jnp.where(keep, part, NEGATIVE)
        for strip in range(2):
            lines = slice(strip * ROWS, (strip + 1) * ROWS)
            peak = scores[lines, 0:128]
            for e in range(1, MAXB):
                peak = jnp.maximum(peak, scores[lines, e * 128 : (e + 1) * 128])
            top = jnp.max(peak, axis=1, keepdims=True) * FACTOR
            total = jnp.zeros((ROWS, BLOCK_POSITIONS), jnp.float32)
            for e in range(MAXB):
                span = slice(e * 128, (e + 1) * 128)
                w = jnp.exp2(scores[lines, span] * FACTOR - top)
                total = total + w
                weights[lines, span] = w.astype(jnp.bfloat16)
            numerator = jnp.dot(weights[lines, :], values[...], preferred_element_type=jnp.float32)
            result = (numerator / jnp.sum(total, axis=1, keepdims=True)).astype(jnp.bfloat16)
            for h in range(GROUP):
                out_ref[2 * b + strip, :, h * HEAD_SIZE : (h + 1) * HEAD_SIZE] = result[h * STRIP : (h + 1) * STRIP]
        return carry

    lax.fori_loop(0, 4, one_block, 0)


def attention(meta, lists, other_lists, q, even, other_even, odd, other_odd, interpret=False):
    smem = pl.BlockSpec(memory_space=pltpu.SMEM)
    vmem = pl.BlockSpec(memory_space=pltpu.VMEM)
    return pl.pallas_call(
        attend,
        out_shape=jax.ShapeDtypeStruct(q.shape, q.dtype),
        in_specs=[smem, smem, smem] + [vmem] * 5,
        out_specs=vmem,
        scratch_shapes=[
            pltpu.VMEM((2 * ROWS, HEAD_SIZE), jnp.bfloat16),
            pltpu.VMEM((KEYS, HEAD_SIZE), jnp.bfloat16),
            pltpu.VMEM((KEYS, HEAD_SIZE), jnp.bfloat16),
            pltpu.VMEM((2 * ROWS, KEYS), jnp.float32),
            pltpu.VMEM((2 * ROWS, KEYS), jnp.bfloat16),
        ],
        compiler_params=pltpu.CompilerParams(vmem_limit_bytes=40 * 2**20),
        cost_estimate=pl.CostEstimate(flops=2**31, bytes_accessed=8 * 2**20, transcendentals=2**22),
        interpret=interpret,
    )(meta, lists, other_lists, q, even, other_even, odd, other_odd)


def swap(array, axis):
    return lax.ppermute(array, axis, [(0, 1), (1, 0)])


def body(queries, keyvals, block_index, block_count):
    lists = jnp.concatenate([block_index, block_count[:, None]], axis=1)
    meta = jnp.stack([lax.axis_index(a) for a in (Z, X, YLO, CORE)]).astype(jnp.int32)
    heads = lax.axis_size(RING)

    chips = lax.axis_size(X)
    sent = keyvals.reshape(2, STRIP, heads, HEAD_SIZE).transpose(2, 0, 1, 3)
    sent = jnp.broadcast_to(sent[None], (chips,) + sent.shape).reshape((chips * heads,) + sent.shape[1:])
    plane = lax.all_to_all(sent, (X,) + RING, split_axis=0, concat_axis=0, tiled=True)
    plane = plane.reshape(chips, 4, 2, 2, STRIP, HEAD_SIZE).transpose(0, 1, 3, 2, 4, 5)
    plane = plane.reshape(chips, 4, 2, HALF, HEAD_SIZE)
    mine = plane[:, 0::2].reshape(2 * chips, 2, HALF, HEAD_SIZE)
    even = lax.all_gather(mine, Z, axis=0, tiled=True)

    queries, plane, lists = lax.optimization_barrier((queries, plane, lists, mine))[:3]
    sent_q = queries.reshape(STRIP, heads, GROUP * HEAD_SIZE).transpose(1, 0, 2)
    q = lax.all_to_all(sent_q, RING, split_axis=0, concat_axis=0, tiled=True)
    other_lists = swap(lists, YLO)
    x = lax.axis_index(X)
    layers = lax.axis_size(Z)
    below = lax.ppermute(plane[chips - 1, 3], Z, [(i, i + 1) for i in range(layers - 1)])
    left = lax.dynamic_index_in_dim(plane, jnp.maximum(x - 1, 0), 0, keepdims=False)[3]
    own = lax.dynamic_index_in_dim(plane, x, 0, keepdims=False)
    odd = jnp.stack([jnp.where(x == 0, below, left), own[1], own[3]])
    other_odd = swap(odd, CORE)
    even, q, other_lists, odd, other_odd = lax.optimization_barrier((even, q, other_lists, odd, other_odd))

    result = attention(meta, lists, other_lists, q, even, swap(even, CORE), odd, other_odd)
    result = lax.all_to_all(result, RING, split_axis=0, concat_axis=0, tiled=True)
    return result.transpose(1, 0, 2).reshape(STRIP, heads * GROUP * HEAD_SIZE)


def solution(mesh):
    pb, kv, ha = mesh.devices.shape
    fine = Mesh(mesh.devices.reshape(pb, kv // 2, 2, ha // 2, 2), (Z, X, YLO, YHI, CORE))
    rows = (Z, X, YLO, YHI, CORE)
    shard = (Z, X, YLO)
    return jax.shard_map(
        body,
        mesh=fine,
        in_specs=(P(rows, None), P(None, rows, None), P(shard, None), P(shard)),
        out_specs=P(rows, None),
        check_vma=False,
    )
```

```python
import math

import jax
import jax.numpy as jnp
from jax import lax
from jax.experimental import pallas as pl
from jax.experimental.pallas import tpu as pltpu
from jax.sharding import Mesh, PartitionSpec as P

HEAD_SIZE = 128
BLOCK_POSITIONS = 128
MAXB = 16
KEYS = MAXB * BLOCK_POSITIONS
HALF = BLOCK_POSITIONS // 2
STRIP = 32
GROUP = 8
ROWS = GROUP * STRIP
ODD = 3
NEGATIVE = -1e30
FACTOR = math.log2(math.e) / math.sqrt(HEAD_SIZE)
Z, X, YLO, YHI, CORE = "z", "x", "ylo", "yhi", "core"
RING = (YLO, YHI)


def attend(core_ref, entries, q_ref, *refs):
    columns, odds = refs[:8], refs[8:10]
    out_ref, table, keys, values, scores, weights, sems = refs[10:]
    core = core_ref[0]
    evens = table.shape[1] - ODD
    per_column = evens // 4
    copies = []

    def bring(source, target):
        copy = pltpu.make_async_copy(source, target, sems.at[len(copies)])
        copy.start()
        copies.append(copy)

    for rc in range(2):
        side = jnp.bitwise_xor(core, rc)
        for source, relative in zip(columns[rc * 4 : rc * 4 + 4], (0, 3 - 2 * side, 1 + 2 * side, 2)):
            bring(source, table.at[rc, pl.ds(relative * per_column, per_column)])
        bring(odds[rc], table.at[rc, pl.ds(evens, ODD)])
    for copy in copies:
        copy.wait()

    cell = lax.broadcasted_iota(jnp.int32, (ROWS, BLOCK_POSITIONS), 1)
    row = lax.broadcasted_iota(jnp.int32, (ROWS, BLOCK_POSITIONS), 0)
    cell_core = jnp.bitwise_xor(cell // HALF, core)
    key_position = (cell % HALF) // STRIP * HALF + cell_core * STRIP + cell % STRIP
    ahead = key_position - core * STRIP - row % STRIP

    def one_block(b, carry):
        count = entries[b, MAXB]
        for e in range(MAXB):
            t = entries[b, e]
            for rc in range(2):
                span = pl.ds(e * BLOCK_POSITIONS + rc * HALF, HALF)
                keys[span, :] = table[rc, t, 0]
                values[span, :] = table[rc, t, 1]
        peaks = []
        for strip in range(2):
            q = jnp.concatenate(
                [q_ref[2 * b + strip, :, h * HEAD_SIZE : (h + 1) * HEAD_SIZE] for h in range(GROUP)], axis=0
            )
            peak = None
            for g in range(MAXB // 2):
                s = lax.dot_general(
                    q,
                    keys[g * 256 : (g + 1) * 256, :],
                    (((1,), (1,)), ((), ())),
                    preferred_element_type=jnp.float32,
                )
                for e in (2 * g, 2 * g + 1):
                    part = s[:, (e % 2) * 128 : (e % 2 + 1) * 128]
                    part = jnp.where(ahead <= strip * HALF if e == 0 else e < count, part, NEGATIVE)
                    scores[strip, e] = part
                    peak = part if peak is None else jnp.maximum(peak, part)
            peaks.append(jnp.max(peak, axis=1, keepdims=True) * FACTOR)
        for strip in range(2):
            total = jnp.zeros((ROWS, BLOCK_POSITIONS), jnp.float32)
            for e in range(MAXB):
                w = jnp.exp2(scores[strip, e] * FACTOR - peaks[strip])
                total = total + w
                weights[strip, :, e * 128 : (e + 1) * 128] = w.astype(jnp.bfloat16)
            numerator = jnp.dot(weights[strip], values[...], preferred_element_type=jnp.float32)
            result = (numerator / jnp.sum(total, axis=1, keepdims=True)).astype(jnp.bfloat16)
            for h in range(GROUP):
                out_ref[2 * b + strip, :, h * HEAD_SIZE : (h + 1) * HEAD_SIZE] = result[h * STRIP : (h + 1) * STRIP]
        return carry

    lax.fori_loop(0, 4, one_block, 0)


def attention(core, entries, q, columns, odds, interpret=False):
    evens = 4 * columns[0].shape[0]
    smem = pl.BlockSpec(memory_space=pltpu.SMEM)
    vmem = pl.BlockSpec(memory_space=pltpu.VMEM)
    hbm = pl.BlockSpec(memory_space=pl.ANY)
    return pl.pallas_call(
        attend,
        out_shape=jax.ShapeDtypeStruct(q.shape, q.dtype),
        in_specs=[smem, smem, vmem] + [hbm] * 10,
        out_specs=vmem,
        scratch_shapes=[
            pltpu.VMEM((2, evens + ODD, 2, HALF, HEAD_SIZE), jnp.bfloat16),
            pltpu.VMEM((KEYS, HEAD_SIZE), jnp.bfloat16),
            pltpu.VMEM((KEYS, HEAD_SIZE), jnp.bfloat16),
            pltpu.VMEM((2, MAXB, ROWS, BLOCK_POSITIONS), jnp.float32),
            pltpu.VMEM((2, ROWS, KEYS), jnp.bfloat16),
            pltpu.SemaphoreType.DMA((10,)),
        ],
        compiler_params=pltpu.CompilerParams(vmem_limit_bytes=40 * 2**20),
        cost_estimate=pl.CostEstimate(flops=2**31, bytes_accessed=8 * 2**20, transcendentals=2**22),
        interpret=interpret,
    )(core, entries, q, *columns, *odds)


def table_entries(z, x, ylo, lists, other_lists, evens):
    listed = jnp.where(ylo == 0, jnp.concatenate([lists, other_lists]), jnp.concatenate([other_lists, lists]))
    j = listed[:, :MAXB]
    relative = jnp.bitwise_and(j // 4 - x, 3)
    even_row = relative * (evens // 4) + j // 16 * 2 + (j // 2) % 2
    odd_row = evens + jnp.clip((j - 4 * (z * 4 + x) + 1) // 2, 0, ODD - 1)
    return jnp.concatenate([jnp.where(j % 2 == 0, even_row, odd_row), listed[:, MAXB:]], axis=1)


def swap(array, axis):
    return lax.ppermute(array, axis, [(0, 1), (1, 0)])


def around(array, axis, by):
    size = lax.axis_size(axis)
    pairs = [(2 * i + c, 2 * ((i + (by, -by)[c]) % size) + c) for i in range(size) for c in range(2)]
    return lax.ppermute(array, (axis, CORE), pairs)


def body(queries, keyvals, block_index, block_count):
    lists = jnp.concatenate([block_index, block_count[:, None]], axis=1)
    z, x, ylo, core = (lax.axis_index(a).astype(jnp.int32) for a in (Z, X, YLO, CORE))
    heads = lax.axis_size(RING)

    sent = keyvals.reshape(2, STRIP, heads, HEAD_SIZE).transpose(2, 0, 1, 3)
    local = lax.all_to_all(sent, RING, split_axis=0, concat_axis=0, tiled=True)
    local, queries = lax.optimization_barrier((local, queries))
    local = local.reshape(4, 2, 2, STRIP, HEAD_SIZE).transpose(0, 2, 1, 3, 4)
    local = local.reshape(4, 2, HALF, HEAD_SIZE)

    summary = jnp.stack([local[0], local[2]])
    copies = jnp.broadcast_to(summary[None], (lax.axis_size(Z),) + summary.shape)
    column = lax.all_to_all(copies, Z, split_axis=0, concat_axis=0, tiled=True)
    column = column.reshape((-1,) + summary.shape[1:])

    sent_q = queries.reshape(STRIP, heads, GROUP * HEAD_SIZE).transpose(1, 0, 2)
    q = lax.all_to_all(sent_q, RING, split_axis=0, concat_axis=0, tiled=True)
    entries = table_entries(z, x, ylo, lists, swap(lists, YLO), 4 * column.shape[0])
    pairs = lax.axis_size((Z, X))
    before = lax.ppermute(local[3], (Z, X), [(i, i + 1) for i in range(pairs - 1)])
    odd = jnp.stack([before, local[1], local[3]])
    other_odd = swap(odd, CORE)
    column, q, entries, odd, other_odd = lax.optimization_barrier((column, q, entries, odd, other_odd))

    first = around(column, X, 1)
    first, column = lax.optimization_barrier((first, column))
    far = around(first, X, 1)
    second = around(column, X, -1)
    columns = [column, first, second, far]
    columns += [swap(piece, CORE) for piece in columns]
    result = attention(core[None], entries, q, columns, [odd, other_odd])
    result = lax.all_to_all(result, RING, split_axis=0, concat_axis=0, tiled=True)
    return result.transpose(1, 0, 2).reshape(STRIP, heads * GROUP * HEAD_SIZE)


def solution(mesh):
    pb, kv, ha = mesh.devices.shape
    fine = Mesh(mesh.devices.reshape(pb, kv // 2, 2, ha // 2, 2), (Z, X, YLO, YHI, CORE))
    rows = (Z, X, YLO, YHI, CORE)
    shard = (Z, X, YLO)
    return jax.shard_map(
        body,
        mesh=fine,
        in_specs=(P(rows, None), P(None, rows, None), P(shard, None), P(shard)),
        out_specs=P(rows, None),
        check_vma=False,
    )
```

```python
import math

import jax
import jax.numpy as jnp
from jax import lax
from jax.experimental import pallas as pl
from jax.experimental.pallas import tpu as pltpu
from jax.sharding import Mesh, PartitionSpec as P

HEAD_SIZE = 128
BLOCK_POSITIONS = 128
MAXB = 16
KEYS = MAXB * BLOCK_POSITIONS
HALF = BLOCK_POSITIONS // 2
STRIP = 32
GROUP = 8
ROWS = GROUP * STRIP
ODD = 3
PLANE = 8
NEGATIVE = -1e30
FACTOR = math.log2(math.e) / math.sqrt(HEAD_SIZE)
Z, X, YLO, YHI, CORE = "z", "x", "ylo", "yhi", "core"
RING = (YLO, YHI)


def attend(place, entries, q_ref, *refs):
    own, odd, rings, swapped = refs[0], refs[1], refs[2:6], refs[6:10]
    out_ref, table, keys, values, scores, weights, sems = refs[10:]
    z, core = place[0], place[1]
    layers = 2 * len(rings)
    evens = layers * PLANE
    copies = []

    def bring(source, target):
        copy = pltpu.make_async_copy(source, target, sems.at[len(copies)])
        copy.start()
        copies.append(copy)

    for half in range(2):
        bring(own.at[half, pl.ds(0, PLANE)], table.at[half, pl.ds(z * PLANE, PLANE)])
        bring(odd.at[half], table.at[half, pl.ds(evens, ODD)])
        for side, pieces in enumerate((rings, swapped)):
            above = jnp.bitwise_xor(core, side)
            for k, piece in enumerate(pieces, 1):
                row = jnp.bitwise_and(z + (2 * above - 1) * k, layers - 1) * PLANE
                size = PLANE
                if k == len(rings):
                    row, size = row + above * (PLANE // 2), PLANE // 2
                bring(piece.at[half, pl.ds(0, size)], table.at[half, pl.ds(row, size)])
                if k == 1:
                    bring(piece.at[half, pl.ds(PLANE, 1)], table.at[half, pl.ds(evens + ODD + above, 1)])
    for copy in copies:
        copy.wait()

    cell = lax.broadcasted_iota(jnp.int32, (ROWS, BLOCK_POSITIONS), 1)
    row = lax.broadcasted_iota(jnp.int32, (ROWS, BLOCK_POSITIONS), 0)
    key_position = (cell % HALF) // STRIP * HALF + cell // HALF * STRIP + cell % STRIP
    ahead = key_position - core * STRIP - row % STRIP

    def one_block(b, carry):
        count = entries[b, MAXB]
        for e in range(MAXB):
            t = entries[b, e]
            for half in range(2):
                span = pl.ds(e * BLOCK_POSITIONS + half * HALF, HALF)
                keys[span, :] = table[half, t, 0]
                values[span, :] = table[half, t, 1]
        peaks = []
        for strip in range(2):
            q = jnp.concatenate(
                [q_ref[2 * b + strip, :, h * HEAD_SIZE : (h + 1) * HEAD_SIZE] for h in range(GROUP)], axis=0
            )
            peak = None
            for g in range(MAXB // 2):
                s = lax.dot_general(
                    q,
                    keys[g * 256 : (g + 1) * 256, :],
                    (((1,), (1,)), ((), ())),
                    preferred_element_type=jnp.float32,
                )
                for e in (2 * g, 2 * g + 1):
                    part = s[:, (e % 2) * 128 : (e % 2 + 1) * 128]
                    part = jnp.where(ahead <= strip * HALF if e == 0 else e < count, part, NEGATIVE)
                    scores[strip, e] = part
                    peak = part if peak is None else jnp.maximum(peak, part)
            peaks.append(jnp.max(peak, axis=1, keepdims=True) * FACTOR)
        for strip in range(2):
            total = jnp.zeros((ROWS, BLOCK_POSITIONS), jnp.float32)
            for e in range(MAXB):
                w = jnp.exp2(scores[strip, e] * FACTOR - peaks[strip])
                total = total + w
                weights[strip, :, e * 128 : (e + 1) * 128] = w.astype(jnp.bfloat16)
            numerator = jnp.dot(weights[strip], values[...], preferred_element_type=jnp.float32)
            result = (numerator / jnp.sum(total, axis=1, keepdims=True)).astype(jnp.bfloat16)
            for h in range(GROUP):
                out_ref[2 * b + strip, :, h * HEAD_SIZE : (h + 1) * HEAD_SIZE] = result[h * STRIP : (h + 1) * STRIP]
        return carry

    lax.fori_loop(0, 4, one_block, 0)


def attention(place, entries, q, own, odd, rings, swapped, interpret=False):
    evens = 2 * len(rings) * PLANE
    smem = pl.BlockSpec(memory_space=pltpu.SMEM)
    vmem = pl.BlockSpec(memory_space=pltpu.VMEM)
    hbm = pl.BlockSpec(memory_space=pl.ANY)
    return pl.pallas_call(
        attend,
        out_shape=jax.ShapeDtypeStruct(q.shape, q.dtype),
        in_specs=[smem, smem, vmem] + [hbm] * 10,
        out_specs=vmem,
        scratch_shapes=[
            pltpu.VMEM((2, evens + ODD + 2, 2, HALF, HEAD_SIZE), jnp.bfloat16),
            pltpu.VMEM((KEYS, HEAD_SIZE), jnp.bfloat16),
            pltpu.VMEM((KEYS, HEAD_SIZE), jnp.bfloat16),
            pltpu.VMEM((2, MAXB, ROWS, BLOCK_POSITIONS), jnp.float32),
            pltpu.VMEM((2, ROWS, KEYS), jnp.bfloat16),
            pltpu.SemaphoreType.DMA((24,)),
        ],
        compiler_params=pltpu.CompilerParams(vmem_limit_bytes=40 * 2**20),
        cost_estimate=pl.CostEstimate(flops=2**31, bytes_accessed=8 * 2**20, transcendentals=2**22),
        interpret=interpret,
    )(place, entries, q, own, odd, *rings, *swapped)


def table_entries(z, x, ylo, lists, other_lists, evens):
    listed = jnp.where(ylo == 0, jnp.concatenate([lists, other_lists]), jnp.concatenate([other_lists, lists]))
    j = listed[:, :MAXB]
    near = jnp.clip((j - 4 * (z * 4 + x) + 1) // 2, 0, ODD - 1)
    odd_row = evens + jnp.where((near == 0) & (x == 0), ODD, near)
    return jnp.concatenate([jnp.where(j % 2 == 0, j // 2, odd_row), listed[:, MAXB:]], axis=1)


def swap(array, axis):
    return lax.ppermute(array, axis, [(0, 1), (1, 0)])


def around(array, axis, by):
    size = lax.axis_size(axis)
    pairs = [(2 * i + c, 2 * ((i + (by, -by)[c]) % size) + c) for i in range(size) for c in range(2)]
    return lax.ppermute(array, (axis, CORE), pairs)


def body(queries, keyvals, block_index, block_count):
    lists = jnp.concatenate([block_index, block_count[:, None]], axis=1)
    z, x, ylo, core = (lax.axis_index(a).astype(jnp.int32) for a in (Z, X, YLO, CORE))
    heads, chips, layers = lax.axis_size(RING), lax.axis_size(X), lax.axis_size(Z)

    sent = keyvals.reshape(2, STRIP, heads, HEAD_SIZE).transpose(2, 0, 1, 3)
    sent = jnp.broadcast_to(sent[None], (chips,) + sent.shape).reshape((chips * heads,) + sent.shape[1:])
    plane = lax.all_to_all(sent, (X,) + RING, split_axis=0, concat_axis=0, tiled=True)
    plane, queries, lists = lax.optimization_barrier((plane, queries, lists))
    plane = plane.reshape(chips, 4, 2, 2, STRIP, HEAD_SIZE).transpose(0, 1, 3, 2, 4, 5)
    plane = plane.reshape(chips, 4, 2, HALF, HEAD_SIZE)

    mine = lax.dynamic_index_in_dim(plane, x, 0, keepdims=False)
    left = lax.dynamic_index_in_dim(plane, jnp.maximum(x - 1, 0), 0, keepdims=False)
    half = jnp.concatenate(
        [
            plane[:, 0::2].reshape(PLANE, 2, HALF, HEAD_SIZE),
            jnp.stack([plane[chips - 1, 3], left[3], mine[1], mine[3]]),
        ]
    )
    other = swap(half, CORE)
    low, high = jnp.where(core == 0, half, other), jnp.where(core == 0, other, half)
    own = jnp.stack([low[: PLANE + 1], high[: PLANE + 1]])
    odd = jnp.stack([low[PLANE + 1 :], high[PLANE + 1 :]])

    sent_q = queries.reshape(STRIP, heads, GROUP * HEAD_SIZE).transpose(1, 0, 2)
    q = lax.all_to_all(sent_q, RING, split_axis=0, concat_axis=0, tiled=True)
    entries = table_entries(z, x, ylo, lists, swap(lists, YLO), layers * PLANE)

    first = around(own, Z, 1)
    second = around(first[:, :PLANE], Z, 1)
    swapped = [swap(first, CORE)]
    second, swapped[0] = lax.optimization_barrier((second, swapped[0]))
    third = around(second, Z, 1)
    swapped.append(swap(second, CORE))
    third, swapped[1], q, entries = lax.optimization_barrier((third, swapped[1], q, entries))
    fourth = around(lax.dynamic_slice_in_dim(third, core * (PLANE // 2), PLANE // 2, 1), Z, 1)
    rings = [first, second, third, fourth]
    swapped += [swap(third, CORE), swap(fourth, CORE)]
    result = attention(jnp.stack([z, core]), entries, q, own, odd, rings, swapped)
    result = lax.all_to_all(result, RING, split_axis=0, concat_axis=0, tiled=True)
    return result.transpose(1, 0, 2).reshape(STRIP, heads * GROUP * HEAD_SIZE)


def solution(mesh):
    pb, kv, ha = mesh.devices.shape
    fine = Mesh(mesh.devices.reshape(pb, kv // 2, 2, ha // 2, 2), (Z, X, YLO, YHI, CORE))
    rows = (Z, X, YLO, YHI, CORE)
    shard = (Z, X, YLO)
    return jax.shard_map(
        body,
        mesh=fine,
        in_specs=(P(rows, None), P(None, rows, None), P(shard, None), P(shard)),
        out_specs=P(rows, None),
        check_vma=False,
    )
```

```python
import math

import jax
import jax.numpy as jnp
from jax import lax
from jax.experimental import pallas as pl
from jax.experimental.pallas import tpu as pltpu
from jax.sharding import Mesh, PartitionSpec as P

HEAD_SIZE = 128
BLOCK_POSITIONS = 128
MAXB = 16
KEYS = MAXB * BLOCK_POSITIONS
HALF = BLOCK_POSITIONS // 2
STRIP = 32
GROUP = 8
ROWS = GROUP * STRIP
ODD = 3
NEGATIVE = -1e30
FACTOR = math.log2(math.e) / math.sqrt(HEAD_SIZE)
Z, X, YLO, YHI, CORE = "z", "x", "ylo", "yhi", "core"
RING = (YLO, YHI)


def attend(core_ref, entries, q_ref, *refs):
    columns = refs[:8]
    out_ref, table, keys, values, scores, weights, sems = refs[8:]
    core = core_ref[0]
    evens = table.shape[1] - ODD
    per_column = evens // 4
    copies = []

    def bring(source, target):
        copy = pltpu.make_async_copy(source, target, sems.at[len(copies)])
        copy.start()
        copies.append(copy)

    for rc in range(2):
        side = jnp.bitwise_xor(core, rc)
        for source, relative in zip(columns[rc * 4 : rc * 4 + 4], (0, 3 - 2 * side, 1 + 2 * side, 2)):
            bring(source.at[pl.ds(0, per_column)], table.at[rc, pl.ds(relative * per_column, per_column)])
        bring(columns[rc * 4].at[pl.ds(per_column, ODD)], table.at[rc, pl.ds(evens, ODD)])
    for copy in copies:
        copy.wait()

    cell = lax.broadcasted_iota(jnp.int32, (ROWS, BLOCK_POSITIONS), 1)
    row = lax.broadcasted_iota(jnp.int32, (ROWS, BLOCK_POSITIONS), 0)
    cell_core = jnp.bitwise_xor(cell // HALF, core)
    key_position = (cell % HALF) // STRIP * HALF + cell_core * STRIP + cell % STRIP
    ahead = key_position - core * STRIP - row % STRIP

    def one_block(b, carry):
        count = entries[b, MAXB]
        for e in range(MAXB):
            t = entries[b, e]
            for rc in range(2):
                span = pl.ds(e * BLOCK_POSITIONS + rc * HALF, HALF)
                keys[span, :] = table[rc, t, 0]
                values[span, :] = table[rc, t, 1]
        peaks = []
        for strip in range(2):
            q = jnp.concatenate(
                [q_ref[2 * b + strip, :, h * HEAD_SIZE : (h + 1) * HEAD_SIZE] for h in range(GROUP)], axis=0
            )
            peak = None
            for g in range(MAXB // 2):
                s = lax.dot_general(
                    q,
                    keys[g * 256 : (g + 1) * 256, :],
                    (((1,), (1,)), ((), ())),
                    preferred_element_type=jnp.float32,
                )
                for e in (2 * g, 2 * g + 1):
                    part = s[:, (e % 2) * 128 : (e % 2 + 1) * 128]
                    part = jnp.where(ahead <= strip * HALF if e == 0 else e < count, part, NEGATIVE)
                    scores[strip, e] = part
                    peak = part if peak is None else jnp.maximum(peak, part)
            peaks.append(jnp.max(peak, axis=1, keepdims=True) * FACTOR)
        for strip in range(2):
            total = jnp.zeros((ROWS, BLOCK_POSITIONS), jnp.float32)
            for e in range(MAXB):
                w = jnp.exp2(scores[strip, e] * FACTOR - peaks[strip])
                total = total + w
                weights[strip, :, e * 128 : (e + 1) * 128] = w.astype(jnp.bfloat16)
            numerator = jnp.dot(weights[strip], values[...], preferred_element_type=jnp.float32)
            result = (numerator / jnp.sum(total, axis=1, keepdims=True)).astype(jnp.bfloat16)
            for h in range(GROUP):
                out_ref[2 * b + strip, :, h * HEAD_SIZE : (h + 1) * HEAD_SIZE] = result[h * STRIP : (h + 1) * STRIP]
        return carry

    lax.fori_loop(0, 4, one_block, 0)


def attention(core, entries, q, columns, interpret=False):
    evens = 4 * columns[1].shape[0]
    smem = pl.BlockSpec(memory_space=pltpu.SMEM)
    vmem = pl.BlockSpec(memory_space=pltpu.VMEM)
    hbm = pl.BlockSpec(memory_space=pl.ANY)
    return pl.pallas_call(
        attend,
        out_shape=jax.ShapeDtypeStruct(q.shape, q.dtype),
        in_specs=[smem, smem, vmem] + [hbm] * 8,
        out_specs=vmem,
        scratch_shapes=[
            pltpu.VMEM((2, evens + ODD, 2, HALF, HEAD_SIZE), jnp.bfloat16),
            pltpu.VMEM((KEYS, HEAD_SIZE), jnp.bfloat16),
            pltpu.VMEM((KEYS, HEAD_SIZE), jnp.bfloat16),
            pltpu.VMEM((2, MAXB, ROWS, BLOCK_POSITIONS), jnp.float32),
            pltpu.VMEM((2, ROWS, KEYS), jnp.bfloat16),
            pltpu.SemaphoreType.DMA((10,)),
        ],
        compiler_params=pltpu.CompilerParams(vmem_limit_bytes=40 * 2**20),
        cost_estimate=pl.CostEstimate(flops=2**31, bytes_accessed=8 * 2**20, transcendentals=2**22),
        interpret=interpret,
    )(core, entries, q, *columns)


def table_entries(z, x, listed, evens):
    j = listed[:, :MAXB]
    relative = jnp.bitwise_and(j // 4 - x, 3)
    even_row = relative * (evens // 4) + j // 16 * 2 + (j // 2) % 2
    odd_row = evens + jnp.clip((j - 4 * (z * 4 + x) + 1) // 2, 0, ODD - 1)
    return jnp.concatenate([jnp.where(j % 2 == 0, even_row, odd_row), listed[:, MAXB:]], axis=1)


def swap(array, axis):
    return lax.ppermute(array, axis, [(0, 1), (1, 0)])


def around(array, axis, by):
    size = lax.axis_size(axis)
    pairs = [(2 * i + c, 2 * ((i + (by, -by)[c]) % size) + c) for i in range(size) for c in range(2)]
    return lax.ppermute(array, (axis, CORE), pairs)


def body(queries, keyvals, block_index, block_count):
    z, x, core = (lax.axis_index(a).astype(jnp.int32) for a in (Z, X, CORE))
    heads = lax.axis_size(RING)

    lists = jnp.concatenate([block_index, block_count[:, None]], axis=1).reshape(1, -1).astype(jnp.bfloat16)
    lists = jnp.pad(lists, ((0, 15), (0, HEAD_SIZE - lists.shape[1])))
    sent = keyvals.reshape(2 * STRIP, heads, HEAD_SIZE).transpose(1, 0, 2)
    sent = jnp.concatenate([sent, jnp.broadcast_to(lists[None], (heads,) + lists.shape)], axis=1)
    received = lax.all_to_all(sent, RING, split_axis=0, concat_axis=0, tiled=True)
    local = received[:, : 2 * STRIP].reshape(4, 2, 2, STRIP, HEAD_SIZE).transpose(0, 2, 1, 3, 4)
    local = local.reshape(4, 2, HALF, HEAD_SIZE)

    summary = jnp.stack([local[0], local[2]])
    copies = jnp.broadcast_to(summary[None], (lax.axis_size(Z),) + summary.shape)
    column = lax.all_to_all(copies, Z, split_axis=0, concat_axis=0, tiled=True)
    column = column.reshape((-1,) + summary.shape[1:])
    column, queries, odd = lax.optimization_barrier((column, queries, local[1::2]))

    first = around(column, X, 1)
    sent_q = queries.reshape(STRIP, heads, GROUP * HEAD_SIZE).transpose(1, 0, 2)
    q = lax.all_to_all(sent_q, RING, split_axis=0, concat_axis=0, tiled=True)
    pairs = lax.axis_size((Z, X))
    before = lax.ppermute(odd[1], (Z, X), [(i, i + 1) for i in range(pairs - 1)])
    first, column, before = lax.optimization_barrier((first, column, before))

    far = around(first, X, 1)
    second = around(column, X, -1)
    own = jnp.concatenate([column, before[None], odd])
    own_swapped = swap(own, CORE)
    first_swapped = swap(first, CORE)
    listed = received[:: heads // 2, 2 * STRIP, : 2 * MAXB + 2].astype(jnp.int32).reshape(4, MAXB + 1)
    entries = table_entries(z, x, listed, 4 * column.shape[0])
    second, q, entries, own_swapped, first_swapped = lax.optimization_barrier(
        (second, q, entries, own_swapped, first_swapped)
    )
    columns = [own, first, second, far, own_swapped, first_swapped, swap(second, CORE), swap(far, CORE)]
    result = attention(core[None], entries, q, columns)
    result = lax.all_to_all(result, RING, split_axis=0, concat_axis=0, tiled=True)
    return result.transpose(1, 0, 2).reshape(STRIP, heads * GROUP * HEAD_SIZE)


def solution(mesh):
    pb, kv, ha = mesh.devices.shape
    fine = Mesh(mesh.devices.reshape(pb, kv // 2, 2, ha // 2, 2), (Z, X, YLO, YHI, CORE))
    rows = (Z, X, YLO, YHI, CORE)
    shard = (Z, X, YLO)
    return jax.shard_map(
        body,
        mesh=fine,
        in_specs=(P(rows, None), P(None, rows, None), P(shard, None), P(shard)),
        out_specs=P(rows, None),
        check_vma=False,
    )
```

```python
import math

import jax
import jax.numpy as jnp
from jax import lax
from jax.experimental import pallas as pl
from jax.experimental.pallas import tpu as pltpu
from jax.sharding import Mesh, PartitionSpec as P

HEAD_SIZE = 128
BLOCK_POSITIONS = 128
MAXB = 16
KEYS = MAXB * BLOCK_POSITIONS
HALF = BLOCK_POSITIONS // 2
STRIP = 32
GROUP = 8
ROWS = GROUP * STRIP
ODD = 3
NEGATIVE = -1e30
FACTOR = math.log2(math.e) / math.sqrt(HEAD_SIZE)
Z, X, YLO, YHI, CORE = "z", "x", "ylo", "yhi", "core"
RING = (YLO, YHI)


def attend(core_ref, entries, q_ref, *refs):
    columns = refs[:8]
    out_ref, keys, values, scores, weights = refs[8:]
    core = core_ref[0]

    cell = lax.broadcasted_iota(jnp.int32, (ROWS, BLOCK_POSITIONS), 1)
    row = lax.broadcasted_iota(jnp.int32, (ROWS, BLOCK_POSITIONS), 0)
    cell_core = jnp.bitwise_xor(cell // HALF, core)
    key_position = (cell % HALF) // STRIP * HALF + cell_core * STRIP + cell % STRIP
    ahead = key_position - core * STRIP - row % STRIP

    def one_block(b, carry):
        count = entries[b, MAXB]
        for e in range(MAXB):
            relative, row = entries[b, e] // 32, entries[b, e] % 32
            inside = jnp.minimum(row, columns[1].shape[0] - 1)
            for rc in range(2):
                own, first, second, far = columns[rc * 4 : rc * 4 + 4]
                side = jnp.bitwise_xor(core, rc)
                span = pl.ds(e * BLOCK_POSITIONS + rc * HALF, HALF)
                for which, target in enumerate((keys, values)):
                    picked = jnp.where(relative == 0, own[row, which], far[inside, which])
                    picked = jnp.where(relative == 3 - 2 * side, first[inside, which], picked)
                    target[span, :] = jnp.where(relative == 1 + 2 * side, second[inside, which], picked)
        peaks = []
        for strip in range(2):
            q = jnp.concatenate(
                [q_ref[2 * b + strip, :, h * HEAD_SIZE : (h + 1) * HEAD_SIZE] for h in range(GROUP)], axis=0
            )
            peak = None
            for g in range(MAXB // 2):
                s = lax.dot_general(
                    q,
                    keys[g * 256 : (g + 1) * 256, :],
                    (((1,), (1,)), ((), ())),
                    preferred_element_type=jnp.float32,
                )
                for e in (2 * g, 2 * g + 1):
                    part = s[:, (e % 2) * 128 : (e % 2 + 1) * 128]
                    part = jnp.where(ahead <= strip * HALF if e == 0 else e < count, part, NEGATIVE)
                    scores[strip, e] = part
                    peak = part if peak is None else jnp.maximum(peak, part)
            peaks.append(jnp.max(peak, axis=1, keepdims=True) * FACTOR)
        for strip in range(2):
            total = jnp.zeros((ROWS, BLOCK_POSITIONS), jnp.float32)
            for e in range(MAXB):
                w = jnp.exp2(scores[strip, e] * FACTOR - peaks[strip])
                total = total + w
                weights[strip, :, e * 128 : (e + 1) * 128] = w.astype(jnp.bfloat16)
            numerator = jnp.dot(weights[strip], values[...], preferred_element_type=jnp.float32)
            result = (numerator / jnp.sum(total, axis=1, keepdims=True)).astype(jnp.bfloat16)
            for h in range(GROUP):
                out_ref[2 * b + strip, :, h * HEAD_SIZE : (h + 1) * HEAD_SIZE] = result[h * STRIP : (h + 1) * STRIP]
        return carry

    lax.fori_loop(0, 4, one_block, 0)


def attention(core, entries, q, columns, interpret=False):
    smem = pl.BlockSpec(memory_space=pltpu.SMEM)
    vmem = pl.BlockSpec(memory_space=pltpu.VMEM)
    return pl.pallas_call(
        attend,
        out_shape=jax.ShapeDtypeStruct(q.shape, q.dtype),
        in_specs=[smem, smem] + [vmem] * 9,
        out_specs=vmem,
        scratch_shapes=[
            pltpu.VMEM((KEYS, HEAD_SIZE), jnp.bfloat16),
            pltpu.VMEM((KEYS, HEAD_SIZE), jnp.bfloat16),
            pltpu.VMEM((2, MAXB, ROWS, BLOCK_POSITIONS), jnp.float32),
            pltpu.VMEM((2, ROWS, KEYS), jnp.bfloat16),
        ],
        compiler_params=pltpu.CompilerParams(vmem_limit_bytes=40 * 2**20),
        cost_estimate=pl.CostEstimate(flops=2**31, bytes_accessed=8 * 2**20, transcendentals=2**22),
        interpret=interpret,
    )(core, entries, q, *columns)


def table_entries(z, x, listed, per_column):
    j = listed[:, :MAXB]
    even = jnp.bitwise_and(j // 4 - x, 3) * 32 + j // 16 * 2 + (j // 2) % 2
    odd = per_column + jnp.clip((j - 4 * (z * 4 + x) + 1) // 2, 0, ODD - 1)
    return jnp.concatenate([jnp.where(j % 2 == 0, even, odd), listed[:, MAXB:]], axis=1)


def swap(array, axis):
    return lax.ppermute(array, axis, [(0, 1), (1, 0)])


def around(array, axis, by):
    size = lax.axis_size(axis)
    pairs = [(2 * i + c, 2 * ((i + (by, -by)[c]) % size) + c) for i in range(size) for c in range(2)]
    return lax.ppermute(array, (axis, CORE), pairs)


def body(queries, keyvals, block_index, block_count):
    z, x, core = (lax.axis_index(a).astype(jnp.int32) for a in (Z, X, CORE))
    heads = lax.axis_size(RING)

    lists = jnp.concatenate([block_index, block_count[:, None]], axis=1).reshape(1, -1).astype(jnp.bfloat16)
    lists = jnp.pad(lists, ((0, 15), (0, HEAD_SIZE - lists.shape[1])))
    sent = keyvals.reshape(2 * STRIP, heads, HEAD_SIZE).transpose(1, 0, 2)
    sent = jnp.concatenate([sent, jnp.broadcast_to(lists[None], (heads,) + lists.shape)], axis=1)
    received = lax.all_to_all(sent, RING, split_axis=0, concat_axis=0, tiled=True)
    local = received[:, : 2 * STRIP].reshape(4, 2, 2, STRIP, HEAD_SIZE).transpose(0, 2, 1, 3, 4)
    local = local.reshape(4, 2, HALF, HEAD_SIZE)

    summary = jnp.stack([local[0], local[2]])
    copies = jnp.broadcast_to(summary[None], (lax.axis_size(Z),) + summary.shape)
    column = lax.all_to_all(copies, Z, split_axis=0, concat_axis=0, tiled=True)
    column = column.reshape((-1,) + summary.shape[1:])
    column, queries, odd = lax.optimization_barrier((column, queries, local[1::2]))

    first = around(column, X, 1)
    sent_q = queries.reshape(STRIP, heads, GROUP * HEAD_SIZE).transpose(1, 0, 2)
    q = lax.all_to_all(sent_q, RING, split_axis=0, concat_axis=0, tiled=True)
    pairs = lax.axis_size((Z, X))
    before = lax.ppermute(odd[1], (Z, X), [(i, i + 1) for i in range(pairs - 1)])
    first, column, before = lax.optimization_barrier((first, column, before))

    far = around(first, X, 1)
    second = around(column, X, -1)
    own = jnp.concatenate([column, before[None], odd])
    own_swapped = swap(own, CORE)
    first_swapped = swap(first, CORE)
    listed = received[:: heads // 2, 2 * STRIP, : 2 * MAXB + 2].astype(jnp.int32).reshape(4, MAXB + 1)
    entries = table_entries(z, x, listed, column.shape[0])
    second, q, entries, own_swapped, first_swapped = lax.optimization_barrier(
        (second, q, entries, own_swapped, first_swapped)
    )
    columns = [own, first, second, far, own_swapped, first_swapped, swap(second, CORE), swap(far, CORE)]
    result = attention(core[None], entries, q, columns)
    result = lax.all_to_all(result, RING, split_axis=0, concat_axis=0, tiled=True)
    return result.transpose(1, 0, 2).reshape(STRIP, heads * GROUP * HEAD_SIZE)


def solution(mesh):
    pb, kv, ha = mesh.devices.shape
    fine = Mesh(mesh.devices.reshape(pb, kv // 2, 2, ha // 2, 2), (Z, X, YLO, YHI, CORE))
    rows = (Z, X, YLO, YHI, CORE)
    shard = (Z, X, YLO)
    return jax.shard_map(
        body,
        mesh=fine,
        in_specs=(P(rows, None), P(None, rows, None), P(shard, None), P(shard)),
        out_specs=P(rows, None),
        check_vma=False,
    )
```

```python
import math

import jax
import jax.numpy as jnp
from jax import lax
from jax.experimental import pallas as pl
from jax.experimental.pallas import tpu as pltpu
from jax.sharding import Mesh, PartitionSpec as P

HEAD_SIZE = 128
BLOCK_POSITIONS = 128
MAXB = 16
KEYS = MAXB * BLOCK_POSITIONS
HALF = BLOCK_POSITIONS // 2
STRIP = 32
GROUP = 8
ROWS = GROUP * STRIP
ODD = 3
NEGATIVE = -1e30
FACTOR = math.log2(math.e) / math.sqrt(HEAD_SIZE)
Z2, Z1, Z0, X, Y0, Y2, Y1, CORE = AXES = ("z2", "z1", "z0", "x", "y0", "y2", "y1", "core")
Z = (Z2, Z1, Z0)
Z_RING = (Z0, Z1, Z2)
Y_RING = (Y0, Y1, Y2)


def attend(core_ref, entries, q_ref, *refs):
    columns = refs[:8]
    out_ref, table, keys, values, scores, peaks, weights, sems = refs[8:]
    core = core_ref[0]
    evens = table.shape[1] - ODD
    per_column = evens // 4
    copies = []

    def bring(source, target):
        copy = pltpu.make_async_copy(source, target, sems.at[len(copies)])
        copy.start()
        copies.append(copy)

    for rc in range(2):
        side = jnp.bitwise_xor(core, rc)
        for source, relative in zip(columns[rc * 4 : rc * 4 + 4], (0, 3 - 2 * side, 1 + 2 * side, 2)):
            bring(source.at[pl.ds(0, per_column)], table.at[rc, pl.ds(relative * per_column, per_column)])
        bring(columns[rc * 4].at[pl.ds(per_column, ODD)], table.at[rc, pl.ds(evens, ODD)])
    for copy in copies:
        copy.wait()

    cell = lax.broadcasted_iota(jnp.int32, (ROWS, BLOCK_POSITIONS), 1)
    row = lax.broadcasted_iota(jnp.int32, (ROWS, BLOCK_POSITIONS), 0)
    cell_core = jnp.bitwise_xor(cell // HALF, core)
    key_position = (cell % HALF) // STRIP * HALF + cell_core * STRIP + cell % STRIP
    ahead = key_position - core * STRIP - row % STRIP

    def one_block(b, carry):
        count = entries[b, MAXB]
        for e in range(MAXB):
            t = entries[b, e]
            for rc in range(2):
                span = pl.ds(e * BLOCK_POSITIONS + rc * HALF, HALF)
                keys[span, :] = table[rc, t, 0]
                values[span, :] = table[rc, t, 1]
        place = b // 2 * 4 + b % 2
        q = jnp.concatenate(
            [
                q_ref[place + 2 * strip, :, h * HEAD_SIZE : (h + 1) * HEAD_SIZE]
                for strip in range(2)
                for h in range(GROUP)
            ],
            axis=0,
        )
        for g in range(MAXB // 2):
            s = lax.dot_general(
                q,
                keys[g * 256 : (g + 1) * 256, :],
                (((1,), (1,)), ((), ())),
                preferred_element_type=jnp.float32,
            )
            for strip in range(2):
                parts = []
                for e in (2 * g, 2 * g + 1):
                    part = s[strip * ROWS : (strip + 1) * ROWS, (e % 2) * 128 : (e % 2 + 1) * 128]
                    part = jnp.where(ahead <= strip * HALF if e == 0 else e < count, part, NEGATIVE)
                    scores[strip, e] = part
                    parts.append(part)
                peak = jnp.maximum(*parts)
                peaks[strip] = peak if g == 0 else jnp.maximum(peaks[strip], peak)
        for strip in range(2):
            top = jnp.max(peaks[strip], axis=1, keepdims=True) * FACTOR
            total = jnp.zeros((ROWS, BLOCK_POSITIONS), jnp.float32)
            for e in range(MAXB):
                w = jnp.exp2(scores[strip, e] * FACTOR - top)
                total = total + w
                weights[strip, :, e * 128 : (e + 1) * 128] = w.astype(jnp.bfloat16)
            numerator = jnp.dot(weights[strip], values[...], preferred_element_type=jnp.float32)
            result = (numerator / jnp.sum(total, axis=1, keepdims=True)).astype(jnp.bfloat16)
            for h in range(GROUP):
                out_ref[place + 2 * strip, :, h * HEAD_SIZE : (h + 1) * HEAD_SIZE] = result[
                    h * STRIP : (h + 1) * STRIP
                ]
        return carry

    lax.fori_loop(0, 4, one_block, 0)


def attention(core, entries, q, columns, interpret=False):
    evens = 4 * columns[1].shape[0]
    smem = pl.BlockSpec(memory_space=pltpu.SMEM)
    vmem = pl.BlockSpec(memory_space=pltpu.VMEM)
    hbm = pl.BlockSpec(memory_space=pl.ANY)
    return pl.pallas_call(
        attend,
        out_shape=jax.ShapeDtypeStruct(q.shape, q.dtype),
        in_specs=[smem, smem, vmem] + [hbm] * 8,
        out_specs=vmem,
        scratch_shapes=[
            pltpu.VMEM((2, evens + ODD, 2, HALF, HEAD_SIZE), jnp.bfloat16),
            pltpu.VMEM((KEYS, HEAD_SIZE), jnp.bfloat16),
            pltpu.VMEM((KEYS, HEAD_SIZE), jnp.bfloat16),
            pltpu.VMEM((2, MAXB, ROWS, BLOCK_POSITIONS), jnp.float32),
            pltpu.VMEM((2, ROWS, BLOCK_POSITIONS), jnp.float32),
            pltpu.VMEM((2, ROWS, KEYS), jnp.bfloat16),
            pltpu.SemaphoreType.DMA((10,)),
        ],
        compiler_params=pltpu.CompilerParams(vmem_limit_bytes=40 * 2**20),
        cost_estimate=pl.CostEstimate(flops=2**31, bytes_accessed=8 * 2**20, transcendentals=2**22),
        interpret=interpret,
    )(core, entries, q, *columns)


def table_entries(z, x, listed, evens):
    j = listed[:, :MAXB]
    relative = jnp.bitwise_and(j // 4 - x, 3)
    layer = j // 64 + j // 32 % 2 * 2 + j // 16 % 2 * 4
    even_row = relative * (evens // 4) + layer * 2 + (j // 2) % 2
    odd_row = evens + jnp.clip((j - 4 * (z * 4 + x) + 1) // 2, 0, ODD - 1)
    return jnp.concatenate([jnp.where(j % 2 == 0, even_row, odd_row), listed[:, MAXB:]], axis=1)


def swap(array, axis):
    return lax.ppermute(array, axis, [(0, 1), (1, 0)])


def around(array, axis, by):
    size = lax.axis_size(axis)
    pairs = [(2 * i + c, 2 * ((i + (by, -by)[c]) % size) + c) for i in range(size) for c in range(2)]
    return lax.ppermute(array, (axis, CORE), pairs)


def body(queries, keyvals, block_index, block_count):
    z, x, core = (lax.axis_index(a).astype(jnp.int32) for a in (Z, X, CORE))
    heads = lax.axis_size(Y_RING)

    lists = jnp.concatenate([block_index, block_count[:, None]], axis=1)
    lists = jnp.pad(lists, ((0, 16 - lists.shape[0]), (0, HEAD_SIZE - lists.shape[1]))).astype(jnp.bfloat16)
    sent = keyvals.reshape(2 * STRIP, heads, HEAD_SIZE).transpose(1, 0, 2)
    sent = jnp.concatenate([sent, jnp.broadcast_to(lists[None], (heads,) + lists.shape)], axis=1)
    received = lax.all_to_all(sent, Y_RING, split_axis=0, concat_axis=0, tiled=True)
    local = received[:, : 2 * STRIP].reshape(2, 2, 2, 2, STRIP, HEAD_SIZE).transpose(0, 2, 3, 1, 4, 5)
    local = local.reshape(4, 2, HALF, HEAD_SIZE)

    summary = jnp.stack([local[0], local[2]])
    copies = jnp.broadcast_to(summary[None], (lax.axis_size(Z),) + summary.shape)
    column = lax.all_to_all(copies, Z_RING, split_axis=0, concat_axis=0, tiled=True)
    column = column.reshape((-1,) + summary.shape[1:])
    column, queries, odd = lax.optimization_barrier((column, queries, local[1::2]))

    first = around(column, X, 1)
    sent_q = queries.reshape(STRIP, heads, GROUP * HEAD_SIZE).transpose(1, 0, 2)
    q = lax.all_to_all(sent_q, Y_RING, split_axis=0, concat_axis=0, tiled=True)
    pairs = lax.axis_size(Z + (X,))
    before = lax.ppermute(odd[1], Z + (X,), [(i, i + 1) for i in range(pairs - 1)])
    first, column, before = lax.optimization_barrier((first, column, before))

    far = around(first, X, 1)
    second = around(column, X, -1)
    own = jnp.concatenate([column, before[None], odd])
    own_swapped = swap(own, CORE)
    first_swapped = swap(first, CORE)
    listed = received[:: heads // 2, 2 * STRIP : 2 * STRIP + 2, : MAXB + 1].astype(jnp.int32).reshape(4, MAXB + 1)
    entries = table_entries(z, x, listed, 4 * column.shape[0])
    second, q, entries, own_swapped, first_swapped = lax.optimization_barrier(
        (second, q, entries, own_swapped, first_swapped)
    )
    columns = [own, first, second, far, own_swapped, first_swapped, swap(second, CORE), swap(far, CORE)]
    result = attention(core[None], entries, q, columns)
    result = lax.all_to_all(result, Y_RING, split_axis=0, concat_axis=0, tiled=True)
    return result.transpose(1, 0, 2).reshape(STRIP, heads * GROUP * HEAD_SIZE)


def solution(mesh):
    rows, shard = AXES, AXES[:5]
    fine = Mesh(mesh.devices.reshape(2, 2, 2, -1, 2, 2, 2, 2), AXES)
    return jax.shard_map(
        body,
        mesh=fine,
        in_specs=(P(rows, None), P(None, rows, None), P(shard, None), P(shard)),
        out_specs=P(rows, None),
        check_vma=False,
    )
```

```python
import math

import jax
import jax.numpy as jnp
from jax import lax
from jax.experimental import pallas as pl
from jax.experimental.pallas import tpu as pltpu
from jax.sharding import Mesh, PartitionSpec as P

HEAD_SIZE = 128
BLOCK_POSITIONS = 128
MAXB = 16
KEYS = MAXB * BLOCK_POSITIONS
HALF = BLOCK_POSITIONS // 2
STRIP = 32
GROUP = 8
ROWS = GROUP * STRIP
ODD = 3
NEGATIVE = -1e30
FACTOR = math.log2(math.e) / math.sqrt(HEAD_SIZE)
Z2, Z1, Z0, X, Y0, Y2, Y1, CORE = AXES = ("z2", "z1", "z0", "x", "y0", "y2", "y1", "core")
Z = (Z2, Z1, Z0)
Z_RING = (Z0, Z1, Z2)
Y_RING = (Y0, Y1, Y2)


def attend(core_ref, entries, q_ref, *refs):
    columns = refs[:8]
    out_ref, table, keys, values, scores, peaks, weights, sems = refs[8:]
    core = core_ref[0]
    evens = table.shape[1] - ODD
    per_column = evens // 4
    copies = []

    def bring(source, target):
        copy = pltpu.make_async_copy(source, target, sems.at[len(copies)])
        copy.start()
        copies.append(copy)

    for rc in range(2):
        side = jnp.bitwise_xor(core, rc)
        for source, relative in zip(columns[rc * 4 : rc * 4 + 4], (0, 3 - 2 * side, 1 + 2 * side, 2)):
            bring(source.at[pl.ds(0, per_column)], table.at[rc, pl.ds(relative * per_column, per_column)])
        bring(columns[rc * 4].at[pl.ds(per_column, ODD)], table.at[rc, pl.ds(evens, ODD)])
    for copy in copies:
        copy.wait()

    cell = lax.broadcasted_iota(jnp.int32, (ROWS, BLOCK_POSITIONS), 1)
    row = lax.broadcasted_iota(jnp.int32, (ROWS, BLOCK_POSITIONS), 0)
    cell_core = jnp.bitwise_xor(cell // HALF, core)
    key_position = (cell % HALF) // STRIP * HALF + cell_core * STRIP + cell % STRIP
    ahead = key_position - core * STRIP - row % STRIP

    def one_block(b, carry):
        count = entries[b, MAXB]
        for e in range(MAXB):
            t = entries[b, e]
            for rc in range(2):
                span = pl.ds(e * BLOCK_POSITIONS + rc * HALF, HALF)
                keys[span, :] = table[rc, t, 0]
                values[span, :] = table[rc, t, 1]
        place = b // 2 * 4 + b % 2
        q = jnp.concatenate(
            [
                q_ref[place + 2 * strip, :, h * HEAD_SIZE : (h + 1) * HEAD_SIZE]
                for strip in range(2)
                for h in range(GROUP)
            ],
            axis=0,
        )
        for g in range(MAXB // 2):
            s = lax.dot_general(
                q,
                keys[g * 256 : (g + 1) * 256, :],
                (((1,), (1,)), ((), ())),
                preferred_element_type=jnp.float32,
            )
            for strip in range(2):
                parts = []
                for e in (2 * g, 2 * g + 1):
                    part = s[strip * ROWS : (strip + 1) * ROWS, (e % 2) * 128 : (e % 2 + 1) * 128]
                    part = jnp.where(ahead <= strip * HALF if e == 0 else e < count, part, NEGATIVE)
                    scores[strip, e] = part
                    parts.append(part)
                peak = jnp.maximum(*parts)
                peaks[strip] = peak if g == 0 else jnp.maximum(peaks[strip], peak)
        for strip in range(2):
            top = jnp.max(peaks[strip], axis=1, keepdims=True) * FACTOR
            total = jnp.zeros((ROWS, BLOCK_POSITIONS), jnp.float32)
            for e in range(MAXB):
                w = jnp.exp2(scores[strip, e] * FACTOR - top)
                total = total + w
                weights[strip, :, e * 128 : (e + 1) * 128] = w.astype(jnp.bfloat16)
            numerator = jnp.dot(weights[strip], values[...], preferred_element_type=jnp.float32)
            result = (numerator / jnp.sum(total, axis=1, keepdims=True)).astype(jnp.bfloat16)
            for h in range(GROUP):
                out_ref[place + 2 * strip, :, h * HEAD_SIZE : (h + 1) * HEAD_SIZE] = result[
                    h * STRIP : (h + 1) * STRIP
                ]
        return carry

    lax.fori_loop(0, 4, one_block, 0)


def attention(core, entries, q, columns, interpret=False):
    evens = 4 * columns[1].shape[0]
    smem = pl.BlockSpec(memory_space=pltpu.SMEM)
    vmem = pl.BlockSpec(memory_space=pltpu.VMEM)
    hbm = pl.BlockSpec(memory_space=pl.ANY)
    return pl.pallas_call(
        attend,
        out_shape=jax.ShapeDtypeStruct(q.shape, q.dtype),
        in_specs=[smem, smem, vmem] + [hbm] * 8,
        out_specs=vmem,
        scratch_shapes=[
            pltpu.VMEM((2, evens + ODD, 2, HALF, HEAD_SIZE), jnp.bfloat16),
            pltpu.VMEM((KEYS, HEAD_SIZE), jnp.bfloat16),
            pltpu.VMEM((KEYS, HEAD_SIZE), jnp.bfloat16),
            pltpu.VMEM((2, MAXB, ROWS, BLOCK_POSITIONS), jnp.float32),
            pltpu.VMEM((2, ROWS, BLOCK_POSITIONS), jnp.float32),
            pltpu.VMEM((2, ROWS, KEYS), jnp.bfloat16),
            pltpu.SemaphoreType.DMA((10,)),
        ],
        compiler_params=pltpu.CompilerParams(vmem_limit_bytes=40 * 2**20),
        cost_estimate=pl.CostEstimate(flops=2**31, bytes_accessed=8 * 2**20, transcendentals=2**22),
        interpret=interpret,
    )(core, entries, q, *columns)


def table_entries(z, x, listed, evens):
    j = listed[:, :MAXB]
    relative = jnp.bitwise_and(j // 4 - x, 3)
    layer = j // 64 + j // 32 % 2 * 2 + j // 16 % 2 * 4
    even_row = relative * (evens // 4) + layer * 2 + (j // 2) % 2
    odd_row = evens + jnp.clip((j - 4 * (z * 4 + x) + 1) // 2, 0, ODD - 1)
    return jnp.concatenate([jnp.where(j % 2 == 0, even_row, odd_row), listed[:, MAXB:]], axis=1)


def swap(array, axis):
    return lax.ppermute(array, axis, [(0, 1), (1, 0)])


def around(array, axis, by):
    size = lax.axis_size(axis)
    pairs = [(2 * i + c, 2 * ((i + (by, -by)[c]) % size) + c) for i in range(size) for c in range(2)]
    return lax.ppermute(array, (axis, CORE), pairs)


def body(queries, keyvals, block_index, block_count):
    z, x, core = (lax.axis_index(a).astype(jnp.int32) for a in (Z, X, CORE))
    heads = lax.axis_size(Y_RING)

    lists = jnp.concatenate([block_index, block_count[:, None]], axis=1)
    lists = jnp.pad(lists, ((0, 16 - lists.shape[0]), (0, HEAD_SIZE - lists.shape[1]))).astype(jnp.bfloat16)
    sent = keyvals.reshape(2 * STRIP, heads, HEAD_SIZE).transpose(1, 0, 2)
    sent = jnp.concatenate([sent, jnp.broadcast_to(lists[None], (heads,) + lists.shape)], axis=1)
    received = lax.all_to_all(sent, Y_RING, split_axis=0, concat_axis=0, tiled=True)
    received, queries = lax.optimization_barrier((received, queries))
    local = received[:, : 2 * STRIP].reshape(2, 2, 2, 2, STRIP, HEAD_SIZE).transpose(0, 2, 3, 1, 4, 5)
    local = local.reshape(4, 2, HALF, HEAD_SIZE)

    summary = jnp.stack([local[0], local[2]])
    copies = jnp.broadcast_to(summary[None], (lax.axis_size(Z),) + summary.shape)
    column = lax.all_to_all(copies, Z_RING, split_axis=0, concat_axis=0, tiled=True)
    column = column.reshape((-1,) + summary.shape[1:])
    sent_q = queries.reshape(STRIP, heads, GROUP * HEAD_SIZE).transpose(1, 0, 2)
    column, sent_q, odd = lax.optimization_barrier((column, sent_q, local[1::2]))

    first = around(column, X, 1)
    q = lax.all_to_all(sent_q, Y_RING, split_axis=0, concat_axis=0, tiled=True)
    pairs = lax.axis_size(Z + (X,))
    before = lax.ppermute(odd[1], Z + (X,), [(i, i + 1) for i in range(pairs - 1)])
    first, column = lax.optimization_barrier((first, column))

    far = around(first, X, 1)
    second = around(column, X, -1)
    own = jnp.concatenate([column, before[None], odd])
    own_swapped = swap(own, CORE)
    first_swapped = swap(first, CORE)
    listed = received[:: heads // 2, 2 * STRIP : 2 * STRIP + 2, : MAXB + 1].astype(jnp.int32).reshape(4, MAXB + 1)
    entries = table_entries(z, x, listed, 4 * column.shape[0])
    second, q, entries, own_swapped, first_swapped = lax.optimization_barrier(
        (second, q, entries, own_swapped, first_swapped)
    )
    columns = [own, first, second, far, own_swapped, first_swapped, swap(second, CORE), swap(far, CORE)]
    result = attention(core[None], entries, q, columns)
    result = lax.all_to_all(result, Y_RING, split_axis=0, concat_axis=0, tiled=True)
    return result.transpose(1, 0, 2).reshape(STRIP, heads * GROUP * HEAD_SIZE)


def solution(mesh):
    rows, shard = AXES, AXES[:5]
    fine = Mesh(mesh.devices.reshape(2, 2, 2, -1, 2, 2, 2, 2), AXES)
    return jax.shard_map(
        body,
        mesh=fine,
        in_specs=(P(rows, None), P(None, rows, None), P(shard, None), P(shard)),
        out_specs=P(rows, None),
        check_vma=False,
    )
```

```python
import math

import jax
import jax.numpy as jnp
from jax import lax
from jax.experimental import pallas as pl
from jax.experimental.pallas import tpu as pltpu
from jax.sharding import Mesh, PartitionSpec as P

HEAD_SIZE = 128
BLOCK_POSITIONS = 128
MAXB = 16
KEYS = MAXB * BLOCK_POSITIONS
HALF = BLOCK_POSITIONS // 2
STRIP = 32
GROUP = 8
ROWS = GROUP * STRIP
ODD = 3
NEGATIVE = -1e30
FACTOR = math.log2(math.e) / math.sqrt(HEAD_SIZE)
Z2, Z1, Z0, X, Y0, Y2, Y1, CORE = AXES = ("z2", "z1", "z0", "x", "y0", "y2", "y1", "core")
Z = (Z2, Z1, Z0)
Z_RING = (Z0, Z1, Z2)
Y_RING = (Y0, Y1, Y2)


def attend(core_ref, entries, q_ref, *refs):
    columns, odds = refs[:8], refs[8:10]
    out_ref, table, keys, values, scores, peaks, weights, sems = refs[10:]
    core = core_ref[0]
    evens = table.shape[1] - ODD
    per_column = evens // 4
    copies = []

    def bring(source, target):
        copy = pltpu.make_async_copy(source, target, sems.at[len(copies)])
        copy.start()
        copies.append(copy)

    for rc in range(2):
        side = jnp.bitwise_xor(core, rc)
        for source, relative in zip(columns[rc * 4 : rc * 4 + 4], (0, 3 - 2 * side, 1 + 2 * side, 2)):
            bring(source, table.at[rc, pl.ds(relative * per_column, per_column)])
        bring(odds[rc], table.at[rc, pl.ds(evens, ODD)])
    for copy in copies:
        copy.wait()

    cell = lax.broadcasted_iota(jnp.int32, (ROWS, BLOCK_POSITIONS), 1)
    row = lax.broadcasted_iota(jnp.int32, (ROWS, BLOCK_POSITIONS), 0)
    cell_core = jnp.bitwise_xor(cell // HALF, core)
    key_position = (cell % HALF) // STRIP * HALF + cell_core * STRIP + cell % STRIP
    ahead = key_position - core * STRIP - row % STRIP

    def one_block(b, carry):
        count = entries[b, MAXB]
        for e in range(MAXB):
            t = entries[b, e]
            for rc in range(2):
                span = pl.ds(e * BLOCK_POSITIONS + rc * HALF, HALF)
                keys[span, :] = table[rc, t, 0]
                values[span, :] = table[rc, t, 1]
        place = b // 2 * 4 + b % 2
        q = jnp.concatenate(
            [
                q_ref[place + 2 * strip, :, h * HEAD_SIZE : (h + 1) * HEAD_SIZE]
                for strip in range(2)
                for h in range(GROUP)
            ],
            axis=0,
        )
        for g in range(MAXB // 2):
            s = lax.dot_general(
                q,
                keys[g * 256 : (g + 1) * 256, :],
                (((1,), (1,)), ((), ())),
                preferred_element_type=jnp.float32,
            )
            for strip in range(2):
                parts = []
                for e in (2 * g, 2 * g + 1):
                    part = s[strip * ROWS : (strip + 1) * ROWS, (e % 2) * 128 : (e % 2 + 1) * 128]
                    part = jnp.where(ahead <= strip * HALF if e == 0 else e < count, part, NEGATIVE)
                    scores[strip, e] = part
                    parts.append(part)
                peak = jnp.maximum(*parts)
                peaks[strip] = peak if g == 0 else jnp.maximum(peaks[strip], peak)
        for strip in range(2):
            top = jnp.max(peaks[strip], axis=1, keepdims=True) * FACTOR
            total = jnp.zeros((ROWS, BLOCK_POSITIONS), jnp.float32)
            for e in range(MAXB):
                w = jnp.exp2(scores[strip, e] * FACTOR - top)
                total = total + w
                weights[strip, :, e * 128 : (e + 1) * 128] = w.astype(jnp.bfloat16)
            numerator = jnp.dot(weights[strip], values[...], preferred_element_type=jnp.float32)
            result = (numerator / jnp.sum(total, axis=1, keepdims=True)).astype(jnp.bfloat16)
            for h in range(GROUP):
                out_ref[place + 2 * strip, :, h * HEAD_SIZE : (h + 1) * HEAD_SIZE] = result[
                    h * STRIP : (h + 1) * STRIP
                ]
        return carry

    lax.fori_loop(0, 4, one_block, 0)


def attention(core, entries, q, columns, odds, interpret=False):
    evens = 4 * columns[1].shape[0]
    smem = pl.BlockSpec(memory_space=pltpu.SMEM)
    vmem = pl.BlockSpec(memory_space=pltpu.VMEM)
    hbm = pl.BlockSpec(memory_space=pl.ANY)
    return pl.pallas_call(
        attend,
        out_shape=jax.ShapeDtypeStruct(q.shape, q.dtype),
        in_specs=[smem, smem, vmem] + [hbm] * 10,
        out_specs=vmem,
        scratch_shapes=[
            pltpu.VMEM((2, evens + ODD, 2, HALF, HEAD_SIZE), jnp.bfloat16),
            pltpu.VMEM((KEYS, HEAD_SIZE), jnp.bfloat16),
            pltpu.VMEM((KEYS, HEAD_SIZE), jnp.bfloat16),
            pltpu.VMEM((2, MAXB, ROWS, BLOCK_POSITIONS), jnp.float32),
            pltpu.VMEM((2, ROWS, BLOCK_POSITIONS), jnp.float32),
            pltpu.VMEM((2, ROWS, KEYS), jnp.bfloat16),
            pltpu.SemaphoreType.DMA((10,)),
        ],
        compiler_params=pltpu.CompilerParams(vmem_limit_bytes=40 * 2**20),
        cost_estimate=pl.CostEstimate(flops=2**31, bytes_accessed=8 * 2**20, transcendentals=2**22),
        interpret=interpret,
    )(core, entries, q, *columns, *odds)


def table_entries(z, x, listed, evens):
    j = listed[:, :MAXB]
    relative = jnp.bitwise_and(j // 4 - x, 3)
    layer = j // 64 + j // 32 % 2 * 2 + j // 16 % 2 * 4
    even_row = relative * (evens // 4) + layer * 2 + (j // 2) % 2
    odd_row = evens + jnp.clip((j - 4 * (z * 4 + x) + 1) // 2, 0, ODD - 1)
    return jnp.concatenate([jnp.where(j % 2 == 0, even_row, odd_row), listed[:, MAXB:]], axis=1)


def swap(array, axis):
    return lax.ppermute(array, axis, [(0, 1), (1, 0)])


def around(array, axis, by):
    size = lax.axis_size(axis)
    pairs = [(2 * i + c, 2 * ((i + (by, -by)[c]) % size) + c) for i in range(size) for c in range(2)]
    return lax.ppermute(array, (axis, CORE), pairs)


def body(queries, keyvals, block_index, block_count):
    z, x, core = (lax.axis_index(a).astype(jnp.int32) for a in (Z, X, CORE))
    heads = lax.axis_size(Y_RING)

    lists = jnp.concatenate([block_index, block_count[:, None]], axis=1)
    lists = jnp.pad(lists, ((0, 16 - lists.shape[0]), (0, HEAD_SIZE - lists.shape[1]))).astype(jnp.bfloat16)
    sent = keyvals.reshape(2 * STRIP, heads, HEAD_SIZE).transpose(1, 0, 2)
    sent = jnp.concatenate([sent, jnp.broadcast_to(lists[None], (heads,) + lists.shape)], axis=1)
    received = lax.all_to_all(sent, Y_RING, split_axis=0, concat_axis=0, tiled=True)
    received, queries = lax.optimization_barrier((received, queries))
    local = received[:, : 2 * STRIP].reshape(2, 2, 2, 2, STRIP, HEAD_SIZE).transpose(0, 2, 3, 1, 4, 5)
    local = local.reshape(4, 2, HALF, HEAD_SIZE)

    summary = jnp.stack([local[0], local[2]])
    copies = jnp.broadcast_to(summary[None], (lax.axis_size(Z),) + summary.shape)
    column = lax.all_to_all(copies, Z_RING, split_axis=0, concat_axis=0, tiled=True)
    column = column.reshape((-1,) + summary.shape[1:])
    sent_q = queries.reshape(STRIP, heads, GROUP * HEAD_SIZE).transpose(1, 0, 2)
    column, sent_q, odd = lax.optimization_barrier((column, sent_q, local[1::2]))

    first = around(column, X, 1)
    q = lax.all_to_all(sent_q, Y_RING, split_axis=0, concat_axis=0, tiled=True)
    pairs = lax.axis_size(Z + (X,))
    before = lax.ppermute(odd[1], Z + (X,), [(i, i + 1) for i in range(pairs - 1)])
    first, column = lax.optimization_barrier((first, column))

    far = around(first, X, 1)
    second = around(column, X, -1)
    listed = received[:: heads // 2, 2 * STRIP : 2 * STRIP + 2, : MAXB + 1].astype(jnp.int32).reshape(4, MAXB + 1)
    entries = table_entries(z, x, listed, 4 * column.shape[0])
    odd = jnp.concatenate([before[None], odd])
    second, q, entries, other_odd = lax.optimization_barrier((second, q, entries, swap(odd, CORE)))
    columns = [column, first, second, far]
    columns += [swap(piece, CORE) for piece in columns]
    result = attention(core[None], entries, q, columns, [odd, other_odd])
    result = lax.all_to_all(result, Y_RING, split_axis=0, concat_axis=0, tiled=True)
    return result.transpose(1, 0, 2).reshape(STRIP, heads * GROUP * HEAD_SIZE)


def solution(mesh):
    rows, shard = AXES, AXES[:5]
    fine = Mesh(mesh.devices.reshape(2, 2, 2, -1, 2, 2, 2, 2), AXES)
    return jax.shard_map(
        body,
        mesh=fine,
        in_specs=(P(rows, None), P(None, rows, None), P(shard, None), P(shard)),
        out_specs=P(rows, None),
        check_vma=False,
    )
```

```python
import math

import jax
import jax.numpy as jnp
from jax import lax
from jax.experimental import pallas as pl
from jax.experimental.pallas import tpu as pltpu
from jax.sharding import Mesh, PartitionSpec as P

HEAD_SIZE = 128
BLOCK_POSITIONS = 128
MAXB = 16
KEYS = MAXB * BLOCK_POSITIONS
HALF = BLOCK_POSITIONS // 2
STRIP = 32
GROUP = 8
ROWS = GROUP * STRIP
ODD = 3
NEGATIVE = -1e30
FACTOR = math.log2(math.e) / math.sqrt(HEAD_SIZE)
Z2, Z1, Z0, X, Y0, Y2, Y1, CORE = AXES = ("z2", "z1", "z0", "x", "y0", "y2", "y1", "core")
Z = (Z2, Z1, Z0)
Z_RING = (Z0, Z1, Z2)
Y_RING = (Y0, Y1, Y2)


def attend(core_ref, entries, q_ref, *refs):
    columns, odds = refs[:8], refs[8:10]
    out_ref, table, keys, values, scores, peaks, weights, sems = refs[10:]
    core = core_ref[0]
    evens = table.shape[1] - ODD
    per_column = evens // 4
    copies = []

    def bring(source, target):
        copy = pltpu.make_async_copy(source, target, sems.at[len(copies)])
        copy.start()
        copies.append(copy)

    for rc in range(2):
        side = jnp.bitwise_xor(core, rc)
        for source, relative in zip(columns[rc * 4 : rc * 4 + 4], (0, 3 - 2 * side, 1 + 2 * side, 2)):
            bring(source, table.at[rc, pl.ds(relative * per_column, per_column)])
        bring(odds[rc], table.at[rc, pl.ds(evens, ODD)])
    for copy in copies:
        copy.wait()

    cell = lax.broadcasted_iota(jnp.int32, (ROWS, BLOCK_POSITIONS), 1)
    row = lax.broadcasted_iota(jnp.int32, (ROWS, BLOCK_POSITIONS), 0)
    cell_core = jnp.bitwise_xor(cell // HALF, core)
    key_position = (cell % HALF) // STRIP * HALF + cell_core * STRIP + cell % STRIP
    ahead = key_position - core * STRIP - row % STRIP

    def one_block(b, carry):
        count = entries[b, MAXB]
        for e in range(MAXB):
            t = entries[b, e]
            for rc in range(2):
                span = pl.ds(e * BLOCK_POSITIONS + rc * HALF, HALF)
                keys[span, :] = table[rc, t, 0]
                values[span, :] = table[rc, t, 1]
        place = b // 2 * 4 + b % 2
        q = jnp.concatenate(
            [
                q_ref[place + 2 * strip, :, h * HEAD_SIZE : (h + 1) * HEAD_SIZE]
                for strip in range(2)
                for h in range(GROUP)
            ],
            axis=0,
        )
        for g in range(MAXB // 2):
            s = lax.dot_general(
                q,
                keys[g * 256 : (g + 1) * 256, :],
                (((1,), (1,)), ((), ())),
                preferred_element_type=jnp.float32,
            )
            for strip in range(2):
                parts = []
                for e in (2 * g, 2 * g + 1):
                    part = s[strip * ROWS : (strip + 1) * ROWS, (e % 2) * 128 : (e % 2 + 1) * 128]
                    part = jnp.where(ahead <= strip * HALF if e == 0 else e < count, part, NEGATIVE)
                    scores[strip, e] = part
                    parts.append(part)
                peak = jnp.maximum(*parts)
                peaks[strip] = peak if g == 0 else jnp.maximum(peaks[strip], peak)
        for strip in range(2):
            top = jnp.max(peaks[strip], axis=1, keepdims=True) * FACTOR
            total = jnp.zeros((ROWS, BLOCK_POSITIONS), jnp.float32)
            for e in range(MAXB):
                w = jnp.exp2(scores[strip, e] * FACTOR - top)
                total = total + w
                weights[strip, :, e * 128 : (e + 1) * 128] = w.astype(jnp.bfloat16)
            numerator = jnp.dot(weights[strip], values[...], preferred_element_type=jnp.float32)
            result = (numerator / jnp.sum(total, axis=1, keepdims=True)).astype(jnp.bfloat16)
            for h in range(GROUP):
                out_ref[place + 2 * strip, :, h * HEAD_SIZE : (h + 1) * HEAD_SIZE] = result[
                    h * STRIP : (h + 1) * STRIP
                ]
        return carry

    lax.fori_loop(0, 4, one_block, 0)


def attention(core, entries, q, columns, odds, interpret=False):
    evens = 4 * columns[1].shape[0]
    smem = pl.BlockSpec(memory_space=pltpu.SMEM)
    vmem = pl.BlockSpec(memory_space=pltpu.VMEM)
    hbm = pl.BlockSpec(memory_space=pl.ANY)
    return pl.pallas_call(
        attend,
        out_shape=jax.ShapeDtypeStruct(q.shape, q.dtype),
        in_specs=[smem, smem, vmem] + [hbm] * 10,
        out_specs=vmem,
        scratch_shapes=[
            pltpu.VMEM((2, evens + ODD, 2, HALF, HEAD_SIZE), jnp.bfloat16),
            pltpu.VMEM((KEYS, HEAD_SIZE), jnp.bfloat16),
            pltpu.VMEM((KEYS, HEAD_SIZE), jnp.bfloat16),
            pltpu.VMEM((2, MAXB, ROWS, BLOCK_POSITIONS), jnp.float32),
            pltpu.VMEM((2, ROWS, BLOCK_POSITIONS), jnp.float32),
            pltpu.VMEM((2, ROWS, KEYS), jnp.bfloat16),
            pltpu.SemaphoreType.DMA((10,)),
        ],
        compiler_params=pltpu.CompilerParams(vmem_limit_bytes=40 * 2**20),
        cost_estimate=pl.CostEstimate(flops=2**31, bytes_accessed=8 * 2**20, transcendentals=2**22),
        interpret=interpret,
    )(core, entries, q, *columns, *odds)


def table_entries(z, x, listed, evens):
    j = listed[:, :MAXB]
    relative = jnp.bitwise_and(j // 4 - x, 3)
    layer = j // 64 + j // 32 % 2 * 2 + j // 16 % 2 * 4
    even_row = relative * (evens // 4) + layer * 2 + (j // 2) % 2
    odd_row = evens + jnp.clip((j - 4 * (z * 4 + x) + 1) // 2, 0, ODD - 1)
    return jnp.concatenate([jnp.where(j % 2 == 0, even_row, odd_row), listed[:, MAXB:]], axis=1)


def swap(array, axis):
    return lax.ppermute(array, axis, [(0, 1), (1, 0)])


def around(array, axis, by):
    size = lax.axis_size(axis)
    pairs = [(2 * i + c, 2 * ((i + (by, -by)[c]) % size) + c) for i in range(size) for c in range(2)]
    return lax.ppermute(array, (axis, CORE), pairs)


def body(queries, keyvals, block_index, block_count):
    z, x, core = (lax.axis_index(a).astype(jnp.int32) for a in (Z, X, CORE))
    heads = lax.axis_size(Y_RING)

    lists = jnp.concatenate([block_index, block_count[:, None]], axis=1)
    lists = jnp.pad(lists, ((0, 16 - lists.shape[0]), (0, HEAD_SIZE - lists.shape[1]))).astype(jnp.bfloat16)
    sent = keyvals.reshape(2 * STRIP, heads, HEAD_SIZE).transpose(1, 0, 2)
    sent = jnp.concatenate([sent, jnp.broadcast_to(lists[None], (heads,) + lists.shape)], axis=1)
    received = lax.all_to_all(sent, Y_RING, split_axis=0, concat_axis=0, tiled=True)
    received, queries = lax.optimization_barrier((received, queries))
    local = received[:, : 2 * STRIP].reshape(2, 2, 2, 2, STRIP, HEAD_SIZE).transpose(0, 2, 3, 1, 4, 5)
    local = local.reshape(4, 2, HALF, HEAD_SIZE)

    summary = jnp.stack([local[0], local[2]])
    copies = jnp.broadcast_to(summary[None], (lax.axis_size(Z),) + summary.shape)
    column = lax.all_to_all(copies, Z_RING, split_axis=0, concat_axis=0, tiled=True)
    column = column.reshape((-1,) + summary.shape[1:])
    sent_q = queries.reshape(STRIP, heads, GROUP * HEAD_SIZE).transpose(1, 0, 2)
    column, sent_q, odd = lax.optimization_barrier((column, sent_q, local[1::2]))

    first = around(column, X, 1)
    q = lax.all_to_all(sent_q, Y_RING, split_axis=0, concat_axis=0, tiled=True)
    pairs = lax.axis_size(Z + (X,))
    before = lax.ppermute(odd[1], Z + (X,), [(i, i + 1) for i in range(pairs - 1)])
    first, column, before = lax.optimization_barrier((first, column, before))

    far = around(first, X, 1)
    second = around(column, X, -1)
    listed = received[:: heads // 2, 2 * STRIP : 2 * STRIP + 2, : MAXB + 1].astype(jnp.int32).reshape(4, MAXB + 1)
    entries = table_entries(z, x, listed, 4 * column.shape[0])
    odd = jnp.concatenate([before[None], odd])
    second, q, entries, other_odd = lax.optimization_barrier((second, q, entries, swap(odd, CORE)))
    columns = [column, first, second, far]
    columns += [swap(piece, CORE) for piece in columns]
    result = attention(core[None], entries, q, columns, [odd, other_odd])
    result = lax.all_to_all(result, Y_RING, split_axis=0, concat_axis=0, tiled=True)
    return result.transpose(1, 0, 2).reshape(STRIP, heads * GROUP * HEAD_SIZE)


def solution(mesh):
    rows, shard = AXES, AXES[:5]
    fine = Mesh(mesh.devices.reshape(2, 2, 2, -1, 2, 2, 2, 2), AXES)
    return jax.shard_map(
        body,
        mesh=fine,
        in_specs=(P(rows, None), P(None, rows, None), P(shard, None), P(shard)),
        out_specs=P(rows, None),
        check_vma=False,
    )
```
